256 devices in a mesh: ctx: 16 (over x, y), tp: 16 (over z, core).
Axes of the slice: x: 4, y: 4, z: 8, core: 2. Of those that a mesh axis runs over, the one named last changes fastest.
Arguments:
- tokens: bfloat16 [32768, 2304], P(('ctx', 'tp')), may hold values from -5 to 5
- query_weight: bfloat16 [2304, 4096], P(None, 'tp'), may hold values from -0.125 to 0.125
- key_weight: bfloat16 [2304, 4096], P(None, 'tp'), may hold values from -0.125 to 0.125
- values_projector_matrix: bfloat16 [2304, 4096], P(None, 'tp'), may hold values from -0.125 to 0.125
- gate_weight: bfloat16 [2304, 4096], P(None, 'tp'), may hold values from -0.125 to 0.125
- beta_weight: bfloat16 [2304, 32], P(None, 'tp'), may hold values from -0.125 to 0.125
- beta_bias: float32 [32], P('tp'), may hold values from -5 to 1
- log_decay: float32 [32768, 4096], P('ctx', 'tp'), may hold values from -1 to 0
- head_gain: float32 [128], replicated, may hold values from 0.25 to 1.75
- output_weight: bfloat16 [4096, 2304], P('tp'), may hold values from -0.09375 to 0.09375
- kv_weight: bfloat16 [2304, 512], replicated, may hold values from -0.125 to 0.125
- kv_gain: float32 [512], replicated, may hold values from 0.25 to 1.75
- owner: int32 [16, 16], P(None, 'tp'), may hold values from 0 to 15, as said below
Outputs:
- mixed: bfloat16 [32768, 2304], P(('ctx', 'tp'))
- latent_cache: bfloat16 [64, 2048, 512], P('ctx', 'tp')
The draws below stay inside these ranges and needn't reach their ends.
Inputs may be any that keep to these rules, and one draw needn't show every extreme that they name: In each column t, each owner receives at most 4 tiles, and some owner receives exactly 4.
All inputs are finite; a program needn't handle non-finite values.
Results may differ from the reference program's by a relative error of at most 0.029.
Values may be sent and summed in bfloat16 or wider, within the bound.
No kernel may reach another device: no remote copies, remote signals or barrier semaphores. Data moves between devices by JAX's collectives and lax.ppermute only.
A program may use at most 128 MiB of HBM per device.

```python
import math
import jax
import jax.numpy as jnp
from jax import lax

D = 2304
H = 32
DK = 128
LAT = 512
TILE = 128
BLK = 128
TILES_DEV = 1
HD = 4096
TOK_DEV = 2048
PROMPT_TOKENS = 32768
CAP = 4
N_CTX = 16
N_TP = 16


def draw_tokens(key, part):
    key = jax.random.fold_in(key, 13)
    first, second, third = jax.random.split(key, 3)
    direction = jax.random.truncated_normal(first, -3.0, 3.0, (1, 1, D))
    signs = jnp.where(jax.random.bernoulli(second, 0.5, (PROMPT_TOKENS // BLK, 1, 1)), 1.0, -1.0)
    noise = jax.random.truncated_normal(third, -3.0, 3.0, (PROMPT_TOKENS, D))
    common = jnp.broadcast_to(signs * direction, (PROMPT_TOKENS // BLK, BLK, D)).reshape(PROMPT_TOKENS, D)
    tokens = (noise + 1.5 * common) / math.sqrt(1.0 + 1.5 * 1.5)
    return tokens.astype(jnp.bfloat16)


def draw_owner(key, part):
    key = jax.random.fold_in(key, 5)
    count = N_CTX * TILES_DEV
    seats = N_CTX * CAP

    def column(col_key):
        first, second, third = jax.random.split(col_key, 3)
        hottest = jax.random.randint(first, (), 0, N_CTX)
        slot_labels = jnp.arange(seats, dtype=jnp.int32)
        scores = jax.random.permutation(second, seats).astype(jnp.int32) + CAP
        scores = jnp.where(slot_labels // CAP == hottest, slot_labels % CAP, scores)
        order = jnp.argsort(scores, stable=True)
        chosen = order[:count] // CAP
        shuffle = jax.random.permutation(third, count)
        return chosen[shuffle].astype(jnp.int32)
    columns = jax.vmap(column)(jax.random.split(key, N_TP))
    return columns.reshape(N_TP, N_CTX, TILES_DEV).transpose(1, 0, 2).reshape(N_CTX, N_TP * TILES_DEV)


def draw_log_decay(key, part):
    key = jax.random.fold_in(key, 9)
    key_vectors = jax.random.split(key, 7)
    hidden_feature_size = H * DK
    slow_share = 0.5
    slow = jax.random.uniform(key_vectors[0], (hidden_feature_size,)) < slow_share
    slow_rate = jnp.exp(jax.random.uniform(key_vectors[1], (hidden_feature_size,), minval=math.log(0.1), maxval=math.log(0.6))) / PROMPT_TOKENS
    fast_rate = jnp.exp(jax.random.uniform(key_vectors[2], (hidden_feature_size,), minval=math.log(1.0 / 50.0), maxval=math.log(1.0 / 20.0)))
    rate = jnp.where(slow, slow_rate, fast_rate)
    device_factor = jnp.exp(jax.random.uniform(key_vectors[3], (N_CTX, 1, hidden_feature_size), minval=math.log(0.5), maxval=math.log(2.0)))
    device_factor = jnp.broadcast_to(device_factor, (N_CTX, TOK_DEV, hidden_feature_size)).reshape(PROMPT_TOKENS, hidden_feature_size)
    rough = jax.random.uniform(key_vectors[4], (PROMPT_TOKENS, hidden_feature_size), minval=0.5, maxval=1.5)
    decay_factor = -(rate[None, :] * device_factor * rough)
    positions = jax.random.randint(key_vectors[5], (3,), 0, PROMPT_TOKENS)
    owner_match = jnp.any(jnp.arange(PROMPT_TOKENS)[:, None] == positions[None, :], axis=1)
    tile_batch_send = jnp.log(jax.random.uniform(key_vectors[6], (PROMPT_TOKENS, hidden_feature_size), minval=0.5, maxval=0.8))
    decay_factor = decay_factor + jnp.where(owner_match[:, None], tile_batch_send, 0.0)
    return decay_factor.astype(jnp.float32)


def block_scale(own_key, extent, shards, least, largest):
    def one(axis_at, parts):
        heights = jax.random.uniform(jax.random.fold_in(jax.random.fold_in(own_key, 6), axis_at), (parts,), jnp.float32, least / len(shards), largest / len(shards))
        return jnp.repeat(jnp.exp(heights), extent[axis_at] // parts).reshape((-1,) + (1,) * (len(extent) - axis_at - 1))

    level = one(*shards[0])
    for cut in shards[1:]:
        level = level * one(*cut)
    return level


def scatter_about(stream_key, extent, width, limit, cuts=(), kind=jnp.bfloat16):
    drawn = width * jax.random.normal(stream_key, extent, jnp.float32)
    if cuts:
        drawn = drawn * block_scale(stream_key, extent, cuts, -0.22, 0.18)
    return jnp.clip(drawn, -limit, limit).astype(kind)


def setup_inputs(seed: int = 0) -> dict:
    key_of = jax.random.split(jax.random.key(seed), 14)
    tokens = draw_tokens(jax.random.fold_in(key_of[13], 71), 0)
    query_weight = scatter_about(key_of[1], (D, HD), D ** -0.5, 0.125, ((1, 16),))
    key_weight = scatter_about(key_of[2], (D, HD), D ** -0.5, 0.125, ((1, 16),))
    values_projector_matrix = scatter_about(key_of[3], (D, HD), D ** -0.5, 0.125, ((1, 16),))
    gate_weight = scatter_about(key_of[4], (D, HD), D ** -0.5, 0.125, ((1, 16),))
    beta_weight = scatter_about(key_of[5], (D, H), D ** -0.5, 0.125, ((1, 16),))
    beta_bias = jnp.clip(-5.0 + 6.0 * jax.random.uniform(key_of[6], (H,), jnp.float32) ** block_scale(key_of[6], (H,), ((0, 16),), -0.2, 0.2), -5.0, 1.0)
    log_decay = draw_log_decay(jax.random.fold_in(key_of[13], 71), 0)
    head_gain = jnp.clip(1.0 + 0.15 * jax.random.normal(key_of[8], (DK,), jnp.float32), 0.25, 1.75)
    output_weight = scatter_about(key_of[9], (HD, D), HD ** -0.5, 0.09375, ((0, 16),))
    kv_weight = scatter_about(key_of[10], (D, LAT), D ** -0.5, 0.125)
    kv_gain = jnp.clip(1.0 + 0.15 * jax.random.normal(key_of[11], (LAT,), jnp.float32), 0.25, 1.75)
    owner = draw_owner(jax.random.fold_in(key_of[13], 71), 0)
    return {"tokens": tokens, "query_weight": query_weight, "key_weight": key_weight, "values_projector_matrix": values_projector_matrix, "gate_weight": gate_weight, "beta_weight": beta_weight, "beta_bias": beta_bias, "log_decay": log_decay, "head_gain": head_gain, "output_weight": output_weight, "kv_weight": kv_weight, "kv_gain": kv_gain, "owner": owner}


EXACT_MATMUL = lax.Precision.HIGHEST
SMALL_GUARD = 1e-06

def unit_rows(vectors):
    return vectors * lax.rsqrt(lax.optimization_barrier(jnp.sum(vectors * vectors, axis=-1, keepdims=True)) + SMALL_GUARD)

def rounded(values):
    return lax.optimization_barrier(values.astype(jnp.bfloat16)).astype(jnp.float32)

def block_terms(queries, key_rows, values, beta_rate, decay_factor):
    hidden_feature_size = queries.shape[-2]
    per_group_channel_size = values.shape[-1]
    cumul = jnp.cumsum(decay_factor, axis=2)
    final = cumul[:, :, -1:, :]
    growth = jnp.exp(cumul)
    key_up = key_rows * growth
    key_down = key_rows * jnp.exp(-cumul)
    query_expansion = queries * growth
    final_key_position = key_rows * jnp.exp(final - cumul)
    row_pos = jnp.arange(hidden_feature_size)[:, None]
    col_pos = jnp.arange(hidden_feature_size)[None, :]
    strict = (row_pos > col_pos).astype(jnp.float32)
    inclusive = (row_pos >= col_pos).astype(jnp.float32)
    rising_low = rounded(key_up)
    falling_low = rounded(key_down)
    query_low = rounded(query_expansion)
    mixing = jnp.einsum('nhik,nhjk->nhij', rising_low, falling_low, precision=EXACT_MATMUL) * strict
    scores = jnp.einsum('nhik,nhjk->nhij', query_low, falling_low, precision=EXACT_MATMUL) * inclusive
    system = jnp.eye(hidden_feature_size, dtype=jnp.float32) + beta_rate[..., None] * mixing
    target = beta_rate[..., None] * jnp.concatenate([values, key_up], axis=-1)
    solved = jax.scipy.linalg.solve_triangular(system, target, lower=True, unit_diagonal=True)
    return (query_expansion, scores, final_key_position, jnp.exp(final[:, :, 0, :]), solved[..., :per_group_channel_size], solved[..., per_group_channel_size:])

def emit_block(recurrent_state, block):
    query_expansion, scores, final_key_position, retain_mask, first_weight, second_weight = block
    state_update = first_weight - jnp.einsum('nrb,nbf->nrf', second_weight, recurrent_state, precision=EXACT_MATMUL)
    layer_output = jnp.einsum('nrb,nbf->nrf', query_expansion, recurrent_state, precision=EXACT_MATMUL)
    layer_output = layer_output + jnp.einsum('hcj,hjv->hcv', scores, state_update, precision=EXACT_MATMUL)
    recurrent_state = retain_mask[:, :, None] * recurrent_state + jnp.einsum('nps,npo->nso', final_key_position, state_update, precision=EXACT_MATMUL)
    return (recurrent_state, layer_output)

def reference(tokens, query_weight, key_weight, values_projector_matrix, gate_weight, beta_weight, beta_bias, log_decay, head_gain, output_weight, kv_weight, kv_gain, owner):
    group_width = HD // N_TP
    group_heads = H // N_TP
    blocks = PROMPT_TOKENS // BLK

    def split(array):
        return array.reshape(blocks, BLK, group_heads, DK).transpose(0, 2, 1, 3)

    def one_group(totals, group_idx):
        start = (group_idx * group_width).astype(jnp.int32)
        head_start = (group_idx * group_heads).astype(jnp.int32)

        def columns(weight):
            return lax.dynamic_slice_in_dim(weight, start, group_width, 1)

        def project(weight):
            return jnp.dot(tokens.astype(jnp.float32), columns(weight).astype(jnp.float32), preferred_element_type=jnp.float32).reshape(PROMPT_TOKENS, group_heads, DK)
        queries = split(unit_rows(project(query_weight)))
        key_rows = split(unit_rows(project(key_weight)))
        values = split(project(values_projector_matrix))
        gate_logit = project(gate_weight)
        beta_logit = jnp.dot(tokens.astype(jnp.float32), lax.dynamic_slice_in_dim(beta_weight, head_start, group_heads, 1).astype(jnp.float32), preferred_element_type=jnp.float32)
        beta_rate = jax.nn.sigmoid(beta_logit + lax.dynamic_slice_in_dim(beta_bias, head_start, group_heads, 0))
        beta_rate = beta_rate.reshape(blocks, BLK, group_heads).transpose(0, 2, 1)
        decay_factor = split(lax.dynamic_slice_in_dim(log_decay, start, group_width, 1))
        terms = block_terms(queries, key_rows, values, beta_rate, decay_factor)
        recurrent_state = jnp.zeros((group_heads, DK, DK), jnp.float32)
        unused, attended = lax.scan(emit_block, recurrent_state, terms)
        attended = attended.transpose(0, 2, 1, 3).reshape(PROMPT_TOKENS, group_heads, DK)
        scale = lax.rsqrt(lax.optimization_barrier(jnp.mean(attended * attended, axis=-1, keepdims=True)) + SMALL_GUARD)
        normed = (attended * scale * head_gain * jax.nn.sigmoid(gate_logit)).reshape(PROMPT_TOKENS, group_width).astype(jnp.bfloat16)
        rows = lax.dynamic_slice_in_dim(output_weight, start, group_width, 0)
        term = lax.optimization_barrier(jnp.dot(normed.astype(jnp.float32), rows.astype(jnp.float32), preferred_element_type=jnp.float32).astype(jnp.bfloat16))
        return (totals + term.astype(jnp.float32), None)
    totals = jnp.zeros((PROMPT_TOKENS, D), jnp.float32)
    totals, unused = lax.scan(one_group, totals, jnp.arange(N_TP, dtype=jnp.int32))
    mixed = totals.astype(jnp.bfloat16)
    latent = jnp.dot(tokens.astype(jnp.float32), kv_weight.astype(jnp.float32), preferred_element_type=jnp.float32)
    latent = (latent * lax.rsqrt(lax.optimization_barrier(jnp.mean(latent * latent, axis=-1, keepdims=True)) + SMALL_GUARD) * kv_gain).astype(jnp.bfloat16)
    count = N_CTX * TILES_DEV
    tiles = latent.reshape(N_CTX, N_TP, TILES_DEV, TILE, LAT).transpose(1, 0, 2, 3, 4).reshape(N_TP, count, TILE, LAT)
    owners = owner.reshape(N_CTX, N_TP, TILES_DEV).transpose(1, 0, 2).reshape(N_TP, count)

    def place(owner_col, tile_column_index):
        same = owner_col[:, None] == owner_col[None, :]
        earlier = jnp.arange(count, dtype=jnp.int32)[None, :] < jnp.arange(count, dtype=jnp.int32)[:, None]
        rank = lax.optimization_barrier(jnp.sum((same & earlier).astype(jnp.int32), axis=1)).astype(jnp.int32)
        receivers = jnp.arange(N_CTX, dtype=jnp.int32)[:, None, None]
        slots = jnp.arange(CAP, dtype=jnp.int32)[None, :, None]
        picker_mask = ((owner_col.astype(jnp.int32)[None, None, :] == receivers) & (rank[None, None, :] == slots)).astype(jnp.float32)
        return jnp.einsum('gyk,kql->gyql', picker_mask, tile_column_index.astype(jnp.float32), precision=EXACT_MATMUL)
    cache = jax.vmap(place)(owners, tiles)
    latent_cache = cache.transpose(1, 2, 0, 3, 4).reshape(N_CTX * CAP, N_TP * TILE, LAT).astype(jnp.bfloat16)
    return (mixed, latent_cache)
```

```python
import functools
import jax
import jax.numpy as jnp
from jax import lax
from jax.experimental import pallas as pl
from jax.experimental.pallas import tpu as pltpu
from jax.sharding import PartitionSpec as P

BLK = 128
GUARD = 1e-06
BF = jnp.bfloat16
F32 = jnp.float32
VMEM_BYTES = 48 * 1024 * 1024


def dot(a, b, contract=((1,), (0,))):
    return lax.dot_general(a, b, (contract, ((), ())), preferred_element_type=F32)


def halves(a):
    high = a.astype(BF)
    return high, (a - high.astype(F32)).astype(BF)


def wide_left(a):
    return jnp.concatenate(halves(a), axis=1)


def wide_right(b):
    row = jnp.concatenate(halves(b), axis=1)
    return jnp.concatenate([row, row], axis=0)


def wide_dot(left, right):
    both = dot(left, right)
    n = both.shape[1] // 2
    return both[:, :n] + both[:, n:]


def indices(shape):
    return lax.broadcasted_iota(jnp.int32, shape, 0), lax.broadcasted_iota(jnp.int32, shape, 1)


def inverses(systems, row, col, exact):
    eye = (row == col).astype(F32)
    joins = (row // 2 == col // 2) & (row > col)
    out = [eye - jnp.where(joins, s, 0.0) for s in systems]
    size = 2
    while size < BLK:
        joins = (row // (2 * size) == col // (2 * size)) & (row // size > col // size)
        parts = [jnp.where(joins, s, 0.0) for s in systems]
        if exact:
            lefts = [wide_left(t) for t in out]
            rights = [wide_right(t) for t in out]
            inner = [wide_dot(wide_left(p), r) for p, r in zip(parts, rights)]
            out = [t - wide_dot(l, wide_right(x)) for t, l, x in zip(out, lefts, inner)]
        else:
            low = [t.astype(BF) for t in out]
            inner = [dot(p.astype(BF), t).astype(BF) for p, t in zip(parts, low)]
            out = [t - dot(l, x) for t, l, x in zip(out, low, inner)]
        size *= 2
    if not exact:
        rest = [-wide_dot(wide_left(s), wide_right(t)) for s, t in zip(systems, out)]
        rest = [(eye - t) + r for t, r in zip(out, rest)]
        out = [t + dot(t.astype(BF), r.astype(BF)) for t, r in zip(out, rest)]
    return out


def terms_kernel(group, at_once, exact, tok, ld, wq, wk, wv, wb, bias, ab_out, po_out, proj, rate):
    rows = tok[...]
    proj[0] = dot(rows, wq[...])
    proj[1] = dot(rows, wk[...])
    proj[2] = dot(rows, wv[...])
    rate[...] = jax.nn.sigmoid(dot(rows, wb[...]) + bias[...])
    row, col = indices((BLK, BLK))
    ones = (row >= col).astype(BF)
    ones2 = jnp.concatenate([ones, ones], axis=1)

    def some(step, carry):
        pairs, wide = [], []
        for j in range(at_once):
            blk = step * at_once + j
            at = pl.ds(pl.multiple_of(blk * BLK, BLK), BLK)
            decay = ld[at, :]
            high = decay.astype(BF)
            rest = decay - high.astype(F32)
            mid = rest.astype(BF)
            low = (rest - mid.astype(F32)).astype(BF)
            cum = dot(ones2, jnp.concatenate([high, mid], axis=0)) + dot(ones, low)
            for h in range(2):
                lanes = slice(h * BLK, (h + 1) * BLK)
                pairs.append((blk, at, h, lanes, cum[:, lanes]))
        systems, targets, scores, ends, firsts, finals = [], [], [], [], [], []
        for blk, at, h, lanes, c in pairs:
            q = proj[0, at, lanes]
            k = proj[1, at, lanes]
            v = proj[2, at, lanes]
            q = q * lax.rsqrt(jnp.sum(q * q, axis=-1, keepdims=True) + GUARD)
            k = k * lax.rsqrt(jnp.sum(k * k, axis=-1, keepdims=True) + GUARD)
            beta = rate[at, h : h + 1]
            final = c[BLK - 1 : BLK, :]
            grow = jnp.exp(c)
            k_up = k * grow
            q_up = q * grow
            k_down = (k * jnp.exp(-c)).astype(BF)
            k_end = k * jnp.exp(final - c)
            gram = dot(jnp.concatenate([k_up, q_up], axis=0).astype(BF), k_down, ((1,), (1,)))
            systems.append(jnp.where(row > col, beta * gram[:BLK], 0.0))
            scores.append(jnp.where(row >= col, gram[BLK:], 0.0).astype(BF))
            targets.append(jnp.concatenate([(beta * k_up).astype(BF), (beta * v).astype(BF)], axis=1))
            ends.append(k_end.T.astype(BF))
            firsts.append(q_up)
            finals.append(jnp.exp(final))
        solved = inverses(systems, row, col, exact)
        solved = [dot(t.astype(BF), g).astype(BF) for t, g in zip(solved, targets)]
        for (blk, at, h, lanes, c), w, s, e, f, last in zip(pairs, solved, scores, ends, firsts, finals):
            both = dot(jnp.concatenate([s, e], axis=0), w)
            po_out[blk, h, :, :BLK] = f - both[:BLK, :BLK]
            po_out[blk, h, :, BLK:] = both[:BLK, BLK:]
            ab_out[blk, h, :, :BLK] = jnp.where(row == col, last, 0.0) - both[BLK:, :BLK]
            ab_out[blk, h, :, BLK:] = both[BLK:, BLK:]
        return carry

    if group == at_once:
        some(0, 0)
    else:
        lax.fori_loop(0, group // at_once, some, 0)


def block_terms(tokens, ld, wq, wk, wv, wb, bias, group=4, at_once=2, exact=True):
    rows, width = tokens.shape
    blocks = rows // BLK
    lanes = wq.shape[1]
    whole = lambda a: pl.BlockSpec(a.shape, lambda i: (0,) * a.ndim)
    out = jax.ShapeDtypeStruct((blocks, 2, BLK, 2 * BLK), F32)
    out_spec = pl.BlockSpec((group, 2, BLK, 2 * BLK), lambda i: (i, 0, 0, 0))
    return pl.pallas_call(
        functools.partial(terms_kernel, group, at_once, exact),
        grid=(blocks // group,),
        in_specs=[
            pl.BlockSpec((group * BLK, width), lambda i: (i, 0)),
            pl.BlockSpec((group * BLK, lanes), lambda i: (i, 0)),
            whole(wq), whole(wk), whole(wv), whole(wb), whole(bias),
        ],
        out_specs=[out_spec, out_spec],
        out_shape=[out, out],
        scratch_shapes=[pltpu.VMEM((3, group * BLK, lanes), F32), pltpu.VMEM((group * BLK, BLK), F32)],
        compiler_params=pltpu.CompilerParams(vmem_limit_bytes=VMEM_BYTES),
        name="block_terms",
    )(tokens, ld, wq, wk, wv, wb, bias)


def narrow_left(a):
    high, low = halves(a)
    return jnp.concatenate([high, low], axis=1), high


def compose(a, x):
    left, high = narrow_left(a)
    x_high, x_low = halves(x)
    return dot(left, jnp.concatenate([x_high, x_high], axis=0)) + dot(high, x_low)


def chain_kernel(group, ab, po, z_out, y_out, x_out, held):
    step = pl.program_id(0)
    row, col = indices((BLK, 2 * BLK))

    @pl.when(step == 0)
    def start():
        for h in range(2):
            held[h] = (row == col).astype(F32)

    x = [held[h] for h in range(2)]
    for j in range(group):
        at = slice(j * BLK, (j + 1) * BLK)
        for h in range(2):
            lanes = slice(h * BLK, (h + 1) * BLK)
            both = dot(po[j, h, :, :BLK].astype(BF), x[h].astype(BF))
            z_out[at, lanes] = both[:, :BLK].astype(BF)
            y_out[at, lanes] = both[:, BLK:] + po[j, h, :, BLK:]
            moved = compose(ab[j, h, :, :BLK], x[h])
            x[h] = jnp.concatenate([moved[:, :BLK], moved[:, BLK:] + ab[j, h, :, BLK:]], axis=1)
    for h in range(2):
        held[h] = x[h]
        x_out[h] = x[h]


def chain(ab, po, group=4):
    blocks = ab.shape[0]
    spec = pl.BlockSpec((group, 2, BLK, 2 * BLK), lambda i: (i, 0, 0, 0))
    rows = pl.BlockSpec((group * BLK, 2 * BLK), lambda i: (i, 0))
    return pl.pallas_call(
        functools.partial(chain_kernel, group),
        grid=(blocks // group,),
        in_specs=[spec, spec],
        out_specs=[rows, rows, pl.BlockSpec((2, BLK, 2 * BLK), lambda i: (0, 0, 0))],
        out_shape=[
            jax.ShapeDtypeStruct((blocks * BLK, 2 * BLK), BF),
            jax.ShapeDtypeStruct((blocks * BLK, 2 * BLK), F32),
            jax.ShapeDtypeStruct((2, BLK, 2 * BLK), F32),
        ],
        scratch_shapes=[pltpu.VMEM((2, BLK, 2 * BLK), F32)],
        compiler_params=pltpu.CompilerParams(vmem_limit_bytes=VMEM_BYTES),
        name="chain",
    )(ab, po)


def side_kernel(place, own, one, two, three, before, total, slots):
    me = place[0]
    for h in range(2):
        slots[0, h] = own[h]
        for d, got in enumerate((one, two, three)):
            slots[d + 1, h] = got[h].astype(F32)
    row, col = indices((BLK, 2 * BLK))
    maps = [None, None]
    for j in range(4):

        @pl.when(me == j)
        def keep():
            for h in range(2):
                before[h] = (row == col).astype(F32) if j == 0 else maps[h]

        at = (me + 4 - j) % 4
        for h in range(2):
            if j == 0:
                maps[h] = slots[at, h]
            else:
                moved = compose(slots[at, h, :, :BLK], maps[h])
                maps[h] = jnp.concatenate(
                    [moved[:, :BLK], moved[:, BLK:] + slots[at, h, :, BLK:]], axis=1
                )
    for h in range(2):
        total[h] = maps[h].astype(BF)


def side_maps(place, own, received):
    whole = pl.BlockSpec(memory_space=pltpu.VMEM)
    return pl.pallas_call(
        side_kernel,
        in_specs=[pl.BlockSpec(memory_space=pltpu.SMEM)] + [whole] * 4,
        out_specs=[whole, whole],
        out_shape=[jax.ShapeDtypeStruct(own.shape, F32), jax.ShapeDtypeStruct(own.shape, BF)],
        scratch_shapes=[pltpu.VMEM((4,) + own.shape, F32)],
        compiler_params=pltpu.CompilerParams(vmem_limit_bytes=VMEM_BYTES),
        name="side_maps",
    )(place, own, *received)


def emit_kernel(place, before, own, one, two, three, z, y, gate, gain, out, slots, state):
    me = place[0]

    @pl.when(pl.program_id(0) == 0)
    def enter():
        for d, got in enumerate((own, one, two, three)):
            slots[d] = got[...]
        for h in range(2):
            s = jnp.zeros((BLK, BLK), F32)
            for j in range(3):
                at = (me + 4 - j) % 4
                moved = slots[at, h, :, BLK:].astype(F32)
                if j > 0:
                    moved = moved + compose(slots[at, h, :, :BLK].astype(F32), s)
                s = jnp.where(j < me, moved, s)
            s = compose(before[h, :, :BLK], s) + before[h, :, BLK:]
            state[h] = s.astype(BF)

    for h in range(2):
        lanes = slice(h * BLK, (h + 1) * BLK)
        a = y[:, lanes] + dot(z[:, lanes], state[h])
        scale = lax.rsqrt(jnp.mean(a * a, axis=-1, keepdims=True) + GUARD)
        a = a * scale * gain[...] * jax.nn.sigmoid(gate[:, lanes].astype(F32))
        out[:, lanes] = a.astype(BF)


def emit(place, before, own, received, z, y, gate, gain, rows=512):
    small = pl.BlockSpec(own.shape, lambda i: (0, 0, 0))
    tall = pl.BlockSpec((rows, 2 * BLK), lambda i: (i, 0))
    return pl.pallas_call(
        emit_kernel,
        grid=(z.shape[0] // rows,),
        in_specs=[pl.BlockSpec(memory_space=pltpu.SMEM)]
        + [small] * 5
        + [tall] * 3
        + [pl.BlockSpec((1, BLK), lambda i: (0, 0))],
        out_specs=tall,
        out_shape=jax.ShapeDtypeStruct(z.shape, BF),
        scratch_shapes=[pltpu.VMEM((4,) + own.shape, BF), pltpu.VMEM((2, BLK, BLK), BF)],
        compiler_params=pltpu.CompilerParams(vmem_limit_bytes=VMEM_BYTES),
        name="emit",
    )(place, before, own, *received, z, y, gate, gain)


def turn(array, axis, pairs):
    return lax.ppermute(array, axis, pairs)


def along_y(d):
    return [(4 * x + y, 4 * x + (y + d) % 4) for x in range(4) for y in range(4)]


def along_x(d):
    return [(4 * x + y, 4 * ((x + d) % 4) + y) for x in range(4) for y in range(4)]


def latent_part(tokens, kv_weight, kv_gain, owner):
    latent = dot(tokens, kv_weight)
    latent = (
        latent * lax.rsqrt(jnp.mean(latent * latent, axis=-1, keepdims=True) + GUARD) * kv_gain
    ).astype(BF)
    owners = owner.reshape(-1)
    count = owners.shape[0]
    order = jnp.arange(count, dtype=jnp.int32)
    same = owners[:, None] == owners[None, :]
    rank = jnp.sum((same & (order[None, :] < order[:, None])).astype(jnp.int32), axis=1)
    slots = jnp.arange(4, dtype=jnp.int32)[:, None]
    picks = ((owners[None, :] == lax.axis_index("ctx")) & (rank[None, :] == slots)).astype(BF)
    tiles = lax.all_gather(latent[None], "ctx", axis=0, tiled=True)
    return jnp.einsum("si,iab->sab", picks, tiles, preferred_element_type=F32).astype(BF)


def body(
    tokens,
    query_weight,
    key_weight,
    values_projector_matrix,
    gate_weight,
    beta_weight,
    beta_bias,
    log_decay,
    head_gain,
    output_weight,
    kv_weight,
    kv_gain,
    owner,
):
    spare = BLK - beta_weight.shape[1]
    rate_weight = jnp.pad(beta_weight, ((0, 0), (0, spare)))
    rate_bias = jnp.pad(beta_bias, (0, spare))[None]
    gathered = lax.all_gather(tokens, "tp", axis=0, tiled=True)
    ab, po = block_terms(
        gathered, log_decay, query_weight, key_weight, values_projector_matrix, rate_weight, rate_bias,
        group=4, at_once=4,
    )
    z, y, maps = chain(ab, po)
    low = maps.astype(BF)
    ctx = lax.axis_index("ctx").astype(jnp.int32)
    received = [turn(low, "ctx", along_y(d)) for d in (1, 2, 3)]
    before, total = side_maps((ctx % 4)[None], maps, received)
    received = [turn(total, "ctx", along_x(d)) for d in (1, 2, 3)]
    gate = dot(gathered, gate_weight).astype(BF)
    normed = emit((ctx // 4)[None], before, total, received, z, y, gate, head_gain[None])
    mixed = lax.psum_scatter(
        dot(normed, output_weight).astype(BF), "tp", scatter_dimension=0, tiled=True
    )
    return mixed, latent_part(tokens, kv_weight, kv_gain, owner)


def solution(mesh):
    in_specs = (
        P(("ctx", "tp"), None),
        P(None, "tp"),
        P(None, "tp"),
        P(None, "tp"),
        P(None, "tp"),
        P(None, "tp"),
        P("tp"),
        P("ctx", "tp"),
        P(),
        P("tp", None),
        P(),
        P(),
        P(None, "tp"),
    )
    out_specs = (P(("ctx", "tp"), None), P("ctx", "tp", None))
    return jax.shard_map(body, mesh=mesh, in_specs=in_specs, out_specs=out_specs, check_vma=False)
```

```python
import functools
import jax
import jax.numpy as jnp
from jax import lax
from jax.experimental import pallas as pl
from jax.experimental.pallas import tpu as pltpu
from jax.sharding import PartitionSpec as P

BLK = 128
GUARD = 1e-06
BF = jnp.bfloat16
F32 = jnp.float32
VMEM_BYTES = 36 * 1024 * 1024


def dot(a, b, contract=((1,), (0,))):
    return lax.dot_general(a, b, (contract, ((), ())), preferred_element_type=F32)


def halves(a):
    high = a.astype(BF)
    return high, (a - high.astype(F32)).astype(BF)


def wide_left(a):
    return jnp.concatenate(halves(a), axis=1)


def wide_right(b):
    row = jnp.concatenate(halves(b), axis=1)
    return jnp.concatenate([row, row], axis=0)


def wide_dot(left, right):
    both = dot(left, right)
    n = both.shape[1] // 2
    return both[:, :n] + both[:, n:]


def indices(shape):
    return lax.broadcasted_iota(jnp.int32, shape, 0), lax.broadcasted_iota(jnp.int32, shape, 1)


def inverses(systems, row, col):
    eye = (row == col).astype(F32)
    joins = (row // 2 == col // 2) & (row > col)
    out = [eye - jnp.where(joins, s, 0.0) for s in systems]
    size = 2
    while size < BLK:
        joins = (row // (2 * size) == col // (2 * size)) & (row // size > col // size)
        parts = [jnp.where(joins, s, 0.0) for s in systems]
        lefts = [wide_left(t) for t in out]
        rights = [wide_right(t) for t in out]
        inner = [wide_dot(wide_left(p), r) for p, r in zip(parts, rights)]
        out = [t - wide_dot(l, wide_right(x)) for t, l, x in zip(out, lefts, inner)]
        size *= 2
    return out


def delta_kernel(group, toks, ld, w, bias, z_out, y_out, x_out, low_out, proj, rate, held):
    rows = jnp.concatenate([toks[j, :BLK] for j in range(group)], axis=0)
    lanes2 = 2 * BLK
    for j in range(3):
        proj[j] = dot(rows, w[:, j * lanes2 : (j + 1) * lanes2])
    rate[...] = jax.nn.sigmoid(dot(rows, w[:, 3 * lanes2 :]) + bias[...])

    @pl.when(pl.program_id(0) == 0)
    def start():
        across, along = indices((BLK, lanes2))
        for h in range(2):
            held[h] = (across == along).astype(F32)

    row, col = indices((BLK, BLK))
    ones = (row >= col).astype(BF)
    ones2 = jnp.concatenate([ones, ones], axis=1)
    pairs = []
    for blk in range(group):
        at = slice(blk * BLK, (blk + 1) * BLK)
        decay = ld[at, :]
        high = decay.astype(BF)
        rest = decay - high.astype(F32)
        mid = rest.astype(BF)
        low = (rest - mid.astype(F32)).astype(BF)
        cum = dot(ones2, jnp.concatenate([high, mid], axis=0)) + dot(ones, low)
        for h in range(2):
            lanes = slice(h * BLK, (h + 1) * BLK)
            pairs.append((blk, at, h, lanes, cum[:, lanes]))
    systems, targets, scores, ends, firsts, finals = [], [], [], [], [], []
    for blk, at, h, lanes, c in pairs:
        q = proj[0, at, lanes]
        k = proj[1, at, lanes]
        v = proj[2, at, lanes]
        q = q * lax.rsqrt(jnp.sum(q * q, axis=-1, keepdims=True) + GUARD)
        k = k * lax.rsqrt(jnp.sum(k * k, axis=-1, keepdims=True) + GUARD)
        beta = rate[at, h : h + 1]
        final = c[BLK - 1 : BLK, :]
        grow = jnp.exp(c)
        k_up = k * grow
        q_up = q * grow
        k_down = (k * jnp.exp(-c)).astype(BF)
        k_end = k * jnp.exp(final - c)
        gram = dot(jnp.concatenate([k_up, q_up], axis=0).astype(BF), k_down, ((1,), (1,)))
        systems.append(jnp.where(row > col, beta * gram[:BLK], 0.0))
        scores.append(jnp.where(row >= col, gram[BLK:], 0.0).astype(BF))
        targets.append(jnp.concatenate([(beta * k_up).astype(BF), (beta * v).astype(BF)], axis=1))
        ends.append(k_end.T.astype(BF))
        firsts.append(q_up)
        finals.append(jnp.exp(final))
    solved = inverses(systems, row, col)
    solved = [dot(t.astype(BF), g).astype(BF) for t, g in zip(solved, targets)]
    earlier, rises, adds, maps = {}, {}, {}, {}
    for (blk, at, h, lanes, c), w_, s, e, f, last in zip(pairs, solved, scores, ends, firsts, finals):
        both = dot(jnp.concatenate([s, e], axis=0), w_)
        p, o = f - both[:BLK, :BLK], both[:BLK, BLK:]
        m, n = jnp.where(row == col, last, 0.0) - both[BLK:, :BLK], both[BLK:, BLK:]
        if blk % 2 == 0:
            earlier[h] = p.astype(BF), o, jnp.concatenate([m, n], axis=1)
        else:
            p0, o0, before = earlier[h]
            seen = dot(p.astype(BF), before.astype(BF))
            rises[blk // 2, h] = jnp.concatenate([p0, seen[:, :BLK].astype(BF)], axis=0)
            adds[blk // 2, h] = jnp.concatenate([o0, seen[:, BLK:] + o], axis=0)
            moved = compose(m, before)
            maps[blk // 2, h] = moved[:, :BLK], moved[:, BLK:] + n
    x = [held[h] for h in range(2)]
    for pair in range(group // 2):
        at = slice(pair * lanes2, (pair + 1) * lanes2)
        for h in range(2):
            lanes = slice(h * BLK, (h + 1) * BLK)
            both = dot(rises[pair, h], x[h].astype(BF))
            z_out[at, lanes] = both[:, :BLK].astype(BF)
            y_out[at, lanes] = both[:, BLK:] + adds[pair, h]
            m, n = maps[pair, h]
            moved = compose(m, x[h])
            x[h] = jnp.concatenate([moved[:, :BLK], moved[:, BLK:] + n], axis=1)
    for h in range(2):
        held[h] = x[h]
        x_out[h] = x[h]
        low_out[h] = x[h].astype(BF)


def narrow_left(a):
    high, low = halves(a)
    return jnp.concatenate([high, low], axis=1), high


def compose(a, x):
    left, high = narrow_left(a)
    x_high, x_low = halves(x)
    return dot(left, jnp.concatenate([x_high, x_high], axis=0)) + dot(high, x_low)


def delta_blocks(tokens, ld, weights, bias, group=4):
    blocks, rows, width = tokens.shape
    lanes = 2 * BLK
    out = pl.BlockSpec((group * BLK, lanes), lambda i: (i, 0))
    last = pl.BlockSpec((2, BLK, lanes), lambda i: (0, 0, 0))
    return pl.pallas_call(
        functools.partial(delta_kernel, group),
        grid=(blocks // group,),
        in_specs=[
            pl.BlockSpec((group, rows, width), lambda i: (i, 0, 0)),
            pl.BlockSpec((group * BLK, lanes), lambda i: (i, 0)),
            pl.BlockSpec(memory_space=pltpu.VMEM),
            pl.BlockSpec(memory_space=pltpu.VMEM),
        ],
        out_specs=[out, out, last, last],
        out_shape=[
            jax.ShapeDtypeStruct((blocks * BLK, lanes), BF),
            jax.ShapeDtypeStruct((blocks * BLK, lanes), F32),
            jax.ShapeDtypeStruct((2, BLK, lanes), F32),
            jax.ShapeDtypeStruct((2, BLK, lanes), BF),
        ],
        scratch_shapes=[
            pltpu.VMEM((3, group * BLK, lanes), F32),
            pltpu.VMEM((group * BLK, BLK), F32),
            pltpu.VMEM((2, BLK, lanes), F32),
        ],
        compiler_params=pltpu.CompilerParams(vmem_limit_bytes=VMEM_BYTES),
        cost_estimate=pl.CostEstimate(
            flops=blocks * BLK * 12 * 10**6, bytes_accessed=blocks * BLK * 12000, transcendentals=0
        ),
        name="delta_blocks",
    )(tokens, ld, weights, bias)


def side_kernel(place, own, one, two, three, before, total, slots):
    me = place[0]
    for h in range(2):
        slots[0, h] = own[h]
        for d, got in enumerate((one, two, three)):
            slots[d + 1, h] = got[h].astype(F32)
    row, col = indices((BLK, 2 * BLK))
    maps = [None, None]
    for j in range(4):

        @pl.when(me == j)
        def keep():
            for h in range(2):
                before[h] = (row == col).astype(F32) if j == 0 else maps[h]

        at = (me + 4 - j) % 4
        for h in range(2):
            if j == 0:
                maps[h] = slots[at, h]
            else:
                moved = compose(slots[at, h, :, :BLK], maps[h])
                maps[h] = jnp.concatenate(
                    [moved[:, :BLK], moved[:, BLK:] + slots[at, h, :, BLK:]], axis=1
                )
    for h in range(2):
        total[h] = maps[h].astype(BF)


def side_maps(place, own, received):
    whole = pl.BlockSpec(own.shape, lambda i: (0, 0, 0))
    return pl.pallas_call(
        side_kernel,
        grid=(1,),
        in_specs=[pl.BlockSpec(memory_space=pltpu.SMEM)] + [whole] * 4,
        out_specs=[whole, whole],
        out_shape=[jax.ShapeDtypeStruct(own.shape, F32), jax.ShapeDtypeStruct(own.shape, BF)],
        scratch_shapes=[pltpu.VMEM((4,) + own.shape, F32)],
        compiler_params=pltpu.CompilerParams(vmem_limit_bytes=VMEM_BYTES),
        name="side_maps",
    )(place, own, *received)


def emit_kernel(group, place, before, own, one, two, three, z, y, gate, gain, out, slots, state):
    me = place[0]

    @pl.when(pl.program_id(0) == 0)
    def enter():
        for d, got in enumerate((own, one, two, three)):
            slots[d] = got[...]
        for h in range(2):
            s = jnp.zeros((BLK, BLK), F32)
            for j in range(3):
                at = (me + 4 - j) % 4
                moved = slots[at, h, :, BLK:].astype(F32)
                if j > 0:
                    moved = moved + compose(slots[at, h, :, :BLK].astype(F32), s)
                s = jnp.where(j < me, moved, s)
            s = compose(before[h, :, :BLK], s) + before[h, :, BLK:]
            state[h] = s.astype(BF)

    for j in range(group):
        at = slice(j * BLK, (j + 1) * BLK)
        for h in range(2):
            lanes = slice(h * BLK, (h + 1) * BLK)
            a = y[at, lanes] + dot(z[at, lanes], state[h])
            scale = lax.rsqrt(jnp.mean(a * a, axis=-1, keepdims=True) + GUARD)
            a = a * scale * gain[...] * jax.nn.sigmoid(gate[j, :BLK, lanes].astype(F32))
            out[at, lanes] = a.astype(BF)


def emit(place, before, own, received, z, y, gate, gain, group=4):
    small = pl.BlockSpec(own.shape, lambda i: (0, 0, 0))
    tall = pl.BlockSpec((group * BLK, 2 * BLK), lambda i: (i, 0))
    return pl.pallas_call(
        functools.partial(emit_kernel, group),
        grid=(z.shape[0] // (group * BLK),),
        in_specs=[pl.BlockSpec(memory_space=pltpu.SMEM)]
        + [small] * 5
        + [tall] * 2
        + [pl.BlockSpec((group,) + gate.shape[1:], lambda i: (i, 0, 0))]
        + [pl.BlockSpec((1, BLK), lambda i: (0, 0))],
        out_specs=tall,
        out_shape=jax.ShapeDtypeStruct(z.shape, BF),
        scratch_shapes=[pltpu.VMEM((4,) + own.shape, BF), pltpu.VMEM((2, BLK, BLK), BF)],
        compiler_params=pltpu.CompilerParams(vmem_limit_bytes=VMEM_BYTES),
        name="emit",
    )(place, before, own, *received, z, y, gate, gain)


def output_kernel(info, a, w, mine, theirs, total):
    core = info[0]
    parts, levels, rows, width = w.shape
    depth = parts * rows
    for i in range(levels):
        at = pl.ds(pl.multiple_of(info[1 + i] * depth, depth), depth)
        more = dot(a[:, at], w[:, i].reshape(depth, width))
        total[...] = more if i == 0 else total[...] + more
    mine[...] = total[pl.ds(pl.multiple_of(core * BLK, BLK), BLK), :]
    theirs[...] = total[pl.ds(pl.multiple_of((1 - core) * BLK, BLK), BLK), :].astype(BF)


def fetch_kernel(far, near, sem):
    copy = pltpu.make_async_copy(far, near, sem)
    copy.start()
    copy.wait()


def fetched(array):
    return pl.pallas_call(
        fetch_kernel,
        in_specs=[pl.BlockSpec(memory_space=pl.ANY)],
        out_specs=pl.BlockSpec(memory_space=pltpu.VMEM),
        out_shape=jax.ShapeDtypeStruct(array.shape, array.dtype),
        scratch_shapes=[pltpu.SemaphoreType.DMA(())],
        compiler_params=pltpu.CompilerParams(vmem_limit_bytes=16 * 1024 * 1024),
        cost_estimate=pl.CostEstimate(flops=0, bytes_accessed=2 * array.size, transcendentals=0),
        name="fetched",
    )(array)


def output_rows(info, normed, weight):
    parts, levels, rows, width = weight.shape
    here = pl.BlockSpec(memory_space=pltpu.VMEM)
    return pl.pallas_call(
        output_kernel,
        in_specs=[pl.BlockSpec(memory_space=pltpu.SMEM), here, here],
        out_specs=[here, here],
        scratch_shapes=[pltpu.VMEM((2 * BLK, width), F32)],
        out_shape=[
            jax.ShapeDtypeStruct((BLK, width), F32),
            jax.ShapeDtypeStruct((BLK, width), BF),
        ],
        compiler_params=pltpu.CompilerParams(vmem_limit_bytes=VMEM_BYTES),
        cost_estimate=pl.CostEstimate(
            flops=4 * BLK * parts * levels * rows * width,
            bytes_accessed=2 * parts * levels * rows * width,
            transcendentals=0,
        ),
        name="output_rows",
    )(info, normed, weight)


def turn(array, axis, pairs):
    return lax.ppermute(array, axis, pairs)


def along_y(d):
    return [(4 * x + y, 4 * x + (y + d) % 4) for x in range(4) for y in range(4)]


def along_x(d):
    return [(4 * x + y, 4 * ((x + d) % 4) + y) for x in range(4) for y in range(4)]


def across():
    return [(t, t ^ 1) for t in range(16)]


def after(array, *others):
    return lax.optimization_barrier((array,) + others)[0]


SAME_CORE = [[2 * z + k for z in range(8)] for k in range(2)]


def latent_rows(tokens, kv_weight, kv_gain):
    latent = dot(tokens, kv_weight)
    scale = lax.rsqrt(jnp.mean(latent * latent, axis=-1, keepdims=True) + GUARD)
    return (latent * scale * kv_gain).astype(BF)


def pick_kernel(info, tile, out):
    out[...] = jnp.where(info[4 + pl.program_id(0)] > 0, tile[...], jnp.zeros_like(out))


def picked(tiles, owner, ctx):
    owners = owner.reshape(-1)
    count = owners.shape[0]
    order = jnp.arange(count, dtype=jnp.int32)
    same = owners[:, None] == owners[None, :]
    rank = jnp.sum((same & (order[None, :] < order[:, None])).astype(jnp.int32), axis=1)
    slots = jnp.arange(4, dtype=jnp.int32)[:, None]
    wanted = ((owners[None, :] == ctx) & (rank[None, :] == slots)).astype(jnp.int32)
    source = jnp.sum(wanted * order[None, :], axis=1)
    place = 4 * ((ctx // 4 - source // 4 + 4) % 4) + (ctx % 4 - source % 4 + 4) % 4
    info = jnp.concatenate([place, jnp.sum(wanted, axis=1)]).astype(jnp.int32)
    shape = tiles.shape[1:]
    return pl.pallas_call(
        pick_kernel,
        grid_spec=pltpu.PrefetchScalarGridSpec(
            num_scalar_prefetch=1,
            grid=(4,),
            in_specs=[pl.BlockSpec((1,) + shape, lambda i, info: (info[i], 0, 0))],
            out_specs=pl.BlockSpec((1,) + shape, lambda i, info: (i, 0, 0)),
        ),
        out_shape=jax.ShapeDtypeStruct((4,) + shape, tiles.dtype),
        compiler_params=pltpu.CompilerParams(vmem_limit_bytes=VMEM_BYTES),
        name="picked",
    )(info, tiles)


def body(
    tokens,
    query_weight,
    key_weight,
    values_projector_matrix,
    gate_weight,
    beta_weight,
    beta_bias,
    log_decay,
    head_gain,
    output_weight,
    kv_weight,
    kv_gain,
    owner,
):
    ctx = lax.axis_index("ctx").astype(jnp.int32)
    tp = lax.axis_index("tp").astype(jnp.int32)
    core = tp % 2
    spare = BLK - beta_weight.shape[1]
    wide = BLK + 16

    part = lax.dynamic_slice_in_dim(output_weight, ctx * 16, 16, 0)
    gathered = lax.all_gather(jnp.concatenate([tokens, part], axis=0), "tp", axis=0)
    weights = jnp.concatenate(
        [query_weight, key_weight, values_projector_matrix, jnp.pad(beta_weight, ((0, 0), (0, spare)))],
        axis=1,
    )
    bias = jnp.pad(beta_bias, (0, spare))[None]
    latent = after(latent_rows(tokens, kv_weight, kv_gain), weights)
    tiles = jnp.stack([latent] + [turn(latent, "ctx", along_y(d)) for d in (1, 2, 3)])
    tiles = jnp.concatenate([tiles] + [turn(tiles, "ctx", along_x(d)) for d in (1, 2, 3)])
    cache = picked(tiles, owner, ctx)
    gathered = after(gathered, cache)
    part = gathered.reshape(8, 2 * wide, -1)
    part = lax.dynamic_slice_in_dim(part, core * wide + BLK, 16, 1).reshape(BLK, -1)
    gathered = after(gathered, part)
    all_parts = lax.all_gather(part, "ctx", axis=0, tiled=True)
    all_parts = all_parts.reshape(16, 8, 16, output_weight.shape[1])

    z, y, maps, low = delta_blocks(gathered, log_decay, weights, bias)
    received = [turn(low, "ctx", along_y(d)) for d in (1, 2, 3)]
    before, total = side_maps((ctx % 4)[None], maps, received)
    received = [turn(total, "ctx", along_x(d)) for d in (1, 2, 3)]
    gate = dot(gathered, gate_weight, ((2,), (0,))).astype(BF)
    normed = emit((ctx // 4)[None], before, total, received, z, y, gate, head_gain[None])

    normed = lax.all_to_all(normed, "tp", 0, 1, tiled=True, axis_index_groups=SAME_CORE)
    info = jnp.stack([core] + [jnp.int32(i) for i in range(8)])
    mine, theirs = output_rows(info, normed, fetched(all_parts))
    theirs = turn(theirs, "tp", across())
    return (mine + theirs.astype(F32)).astype(BF), cache


def solution(mesh):
    in_specs = (
        P(("ctx", "tp"), None),
        P(None, "tp"),
        P(None, "tp"),
        P(None, "tp"),
        P(None, "tp"),
        P(None, "tp"),
        P("tp"),
        P("ctx", "tp"),
        P(),
        P("tp", None),
        P(),
        P(),
        P(None, "tp"),
    )
    out_specs = (P(("ctx", "tp"), None), P("ctx", "tp", None))
    return jax.shard_map(body, mesh=mesh, in_specs=in_specs, out_specs=out_specs, check_vma=False)
```

```python
import functools
import jax
import jax.numpy as jnp
from jax import lax
from jax.experimental import pallas as pl
from jax.experimental.pallas import tpu as pltpu
from jax.sharding import PartitionSpec as P

BLK = 128
GUARD = 1e-06
BF = jnp.bfloat16
F32 = jnp.float32
VMEM_BYTES = 36 * 1024 * 1024


def dot(a, b, contract=((1,), (0,))):
    return lax.dot_general(a, b, (contract, ((), ())), preferred_element_type=F32)


def halves(a):
    high = a.astype(BF)
    return high, (a - high.astype(F32)).astype(BF)


def wide_left(a):
    return jnp.concatenate(halves(a), axis=1)


def wide_right(b):
    row = jnp.concatenate(halves(b), axis=1)
    return jnp.concatenate([row, row], axis=0)


def wide_dot(left, right):
    both = dot(left, right)
    n = both.shape[1] // 2
    return both[:, :n] + both[:, n:]


def indices(shape):
    return lax.broadcasted_iota(jnp.int32, shape, 0), lax.broadcasted_iota(jnp.int32, shape, 1)


def inverses(systems, row, col):
    eye = (row == col).astype(F32)
    joins = (row // 2 == col // 2) & (row > col)
    out = [eye - jnp.where(joins, s, 0.0) for s in systems]
    size = 2
    while size < BLK:
        joins = (row // (2 * size) == col // (2 * size)) & (row // size > col // size)
        parts = [jnp.where(joins, s, 0.0) for s in systems]
        lefts = [wide_left(t) for t in out]
        rights = [wide_right(t) for t in out]
        inner = [wide_dot(wide_left(p), r) for p, r in zip(parts, rights)]
        out = [t - wide_dot(l, wide_right(x)) for t, l, x in zip(out, lefts, inner)]
        size *= 2
    return out


def running(decay, ones):
    high = decay.astype(BF)
    rest = decay - high.astype(F32)
    mid = rest.astype(BF)
    low = (rest - mid.astype(F32)).astype(BF)
    both = dot(jnp.concatenate([ones, ones], axis=1), jnp.concatenate([high, mid], axis=0))
    return both + dot(ones, low)


def unit(rows):
    return rows * lax.rsqrt(jnp.sum(rows * rows, axis=-1, keepdims=True) + GUARD)


def delta_kernel(
    group, toks, ld, wk, wv, wb, bias, k_out, w_out, s_out, x_out, low_out, proj, rate, held
):
    first = pl.program_id(0) == 0
    lanes2 = 2 * BLK
    rows = toks[...]
    proj[0] = dot(rows, wk[...])
    proj[1] = dot(rows, wv[...])
    rate[...] = jax.nn.sigmoid(dot(rows, wb[...]) + bias[...])

    @pl.when(first)
    def start():
        across, along = indices((BLK, lanes2))
        for h in range(2):
            held[h] = (across == along).astype(F32)

    row, col = indices((BLK, BLK))
    ones = (row >= col).astype(BF)
    pairs = []
    for blk in range(group):
        at = slice(blk * BLK, (blk + 1) * BLK)
        decay = ld[at, :]
        cum = running(decay, ones)
        for h in range(2):
            lanes = slice(h * BLK, (h + 1) * BLK)
            pairs.append((blk, at, h, lanes, cum[:, lanes]))
    systems, targets, ends, finals = [], [], [], []
    for blk, at, h, lanes, c in pairs:
        k = unit(proj[0, at, lanes])
        v = proj[1, at, lanes]
        beta = rate[at, h : h + 1]
        final = c[BLK - 1 : BLK, :]
        grow = jnp.exp(c)
        k_up = k * grow
        k_down = (k * jnp.exp(-c)).astype(BF)
        k_end = k * jnp.exp(final - c)
        k_out[at, lanes] = k_down
        gram = dot(k_up.astype(BF), k_down, ((1,), (1,)))
        systems.append(jnp.where(row > col, beta * gram, 0.0))
        targets.append(jnp.concatenate([(beta * k_up).astype(BF), (beta * v).astype(BF)], axis=1))
        ends.append(k_end.T.astype(BF))
        finals.append(jnp.exp(final))
    solved = inverses(systems, row, col)
    solved = [dot(t.astype(BF), g).astype(BF) for t, g in zip(solved, targets)]
    maps = {}
    for (blk, at, h, lanes, c), w_, e, last in zip(pairs, solved, ends, finals):
        w_out[blk, h] = w_
        both = dot(e, w_)
        m, n = jnp.where(row == col, last, 0.0) - both[:, :BLK], both[:, BLK:]
        maps[blk, h] = m, n
    joint = {}
    for pair in range(group // 2):
        for h in range(2):
            joint[pair, h] = follow(maps[2 * pair + 1, h], jnp.concatenate(maps[2 * pair, h], axis=1))
    x = [held[h] for h in range(2)]
    for pair in range(group // 2):
        for h in range(2):
            s_out[2 * pair, h] = x[h].astype(BF)
            s_out[2 * pair + 1, h] = follow(maps[2 * pair, h], x[h]).astype(BF)
            m, n = joint[pair, h][:, :BLK], joint[pair, h][:, BLK:]
            x[h] = follow((m, n), x[h])
    for h in range(2):
        held[h] = x[h]
        x_out[h] = x[h]
        low_out[h] = x[h].astype(BF)


def narrow_left(a):
    high, low = halves(a)
    return jnp.concatenate([high, low], axis=1), high


def compose(a, x):
    left, high = narrow_left(a)
    x_high, x_low = halves(x)
    return dot(left, jnp.concatenate([x_high, x_high], axis=0)) + dot(high, x_low)


def follow(step, x):
    moved = compose(step[0], x)
    return jnp.concatenate([moved[:, :BLK], moved[:, BLK:] + step[1]], axis=1)


def delta_blocks(tokens, ld, wk, wv, wb, bias, group=4):
    rows, width = tokens.shape
    blocks = rows // BLK
    lanes = 2 * BLK
    tall = pl.BlockSpec((group * BLK, lanes), lambda i: (i, 0))
    square = pl.BlockSpec((group, 2, BLK, lanes), lambda i: (i, 0, 0, 0))
    last = pl.BlockSpec((2, BLK, lanes), lambda i: (0, 0, 0))
    whole = lambda a: pl.BlockSpec(a.shape, lambda i: (0, 0))
    return pl.pallas_call(
        functools.partial(delta_kernel, group),
        grid=(blocks // group,),
        in_specs=[
            pl.BlockSpec((group * BLK, width), lambda i: (i, 0)),
            tall,
            whole(wk),
            whole(wv),
            whole(wb),
            whole(bias),
        ],
        out_specs=[tall, square, square, last, last],
        out_shape=[
            jax.ShapeDtypeStruct((rows, lanes), BF),
            jax.ShapeDtypeStruct((blocks, 2, BLK, lanes), BF),
            jax.ShapeDtypeStruct((blocks, 2, BLK, lanes), BF),
            jax.ShapeDtypeStruct((2, BLK, lanes), F32),
            jax.ShapeDtypeStruct((2, BLK, lanes), BF),
        ],
        scratch_shapes=[
            pltpu.VMEM((2, group * BLK, lanes), F32),
            pltpu.VMEM((group * BLK, BLK), F32),
            pltpu.VMEM((2, BLK, lanes), F32),
        ],
        compiler_params=pltpu.CompilerParams(vmem_limit_bytes=VMEM_BYTES),
        cost_estimate=pl.CostEstimate(
            flops=rows * 12 * 10**6, bytes_accessed=rows * 12000, transcendentals=0
        ),
        name="delta_blocks",
    )(tokens, ld, wk, wv, wb, bias)


def rise_kernel(group, q, ld, k, w, s, z_out, y_out):
    row, col = indices((BLK, BLK))
    ones = (row >= col).astype(BF)
    todo = [(j, h) for j in range(group) for h in range(2)]
    places = [(slice(j * BLK, (j + 1) * BLK), slice(h * BLK, (h + 1) * BLK)) for j, h in todo]
    grow = [jnp.exp(running(ld[j * BLK : (j + 1) * BLK], ones)) for j in range(group)]
    ups = [unit(q[p]) * grow[j][:, p[1]] for p, (j, h) in zip(places, todo)]
    grams = [dot(u.astype(BF), k[p], ((1,), (1,))) for u, p in zip(ups, places)]
    grams = [jnp.where(row >= col, g, 0.0).astype(BF) for g in grams]
    both = [dot(g, w[j, h]) for g, (j, h) in zip(grams, todo)]
    rises = [(u - b[:, :BLK]).astype(BF) for u, b in zip(ups, both)]
    for p, b, r, (j, h) in zip(places, both, rises, todo):
        seen = dot(r, s[j, h])
        z_out[p] = seen[:, :BLK].astype(BF)
        y_out[p] = seen[:, BLK:] + b[:, BLK:]


def rise(q, ld, k, w, s, group=4):
    rows, lanes = q.shape
    tall = pl.BlockSpec((group * BLK, lanes), lambda i: (i, 0))
    square = pl.BlockSpec((group,) + w.shape[1:], lambda i: (i, 0, 0, 0))
    return pl.pallas_call(
        functools.partial(rise_kernel, group),
        grid=(rows // (group * BLK),),
        in_specs=[tall, tall, tall, square, square],
        out_specs=[tall, tall],
        out_shape=[jax.ShapeDtypeStruct((rows, lanes), BF), jax.ShapeDtypeStruct((rows, lanes), F32)],
        compiler_params=pltpu.CompilerParams(vmem_limit_bytes=VMEM_BYTES),
        cost_estimate=pl.CostEstimate(
            flops=rows * 3 * 10**6, bytes_accessed=rows * 6000, transcendentals=0
        ),
        name="rise",
    )(q, ld, k, w, s)


def side_kernel(place, own, one, two, three, before, total, slots):
    me = place[0]
    for h in range(2):
        slots[0, h] = own[h]
        for d, got in enumerate((one, two, three)):
            slots[d + 1, h] = got[h].astype(F32)
    row, col = indices((BLK, 2 * BLK))
    maps = [None, None]
    for j in range(4):

        @pl.when(me == j)
        def keep():
            for h in range(2):
                before[h] = (row == col).astype(F32) if j == 0 else maps[h]

        at = (me + 4 - j) % 4
        for h in range(2):
            if j == 0:
                maps[h] = slots[at, h]
            else:
                moved = compose(slots[at, h, :, :BLK], maps[h])
                maps[h] = jnp.concatenate(
                    [moved[:, :BLK], moved[:, BLK:] + slots[at, h, :, BLK:]], axis=1
                )
    for h in range(2):
        total[h] = maps[h].astype(BF)


def side_maps(place, own, received):
    whole = pl.BlockSpec(own.shape, lambda i: (0, 0, 0))
    return pl.pallas_call(
        side_kernel,
        grid=(1,),
        in_specs=[pl.BlockSpec(memory_space=pltpu.SMEM)] + [whole] * 4,
        out_specs=[whole, whole],
        out_shape=[jax.ShapeDtypeStruct(own.shape, F32), jax.ShapeDtypeStruct(own.shape, BF)],
        scratch_shapes=[pltpu.VMEM((4,) + own.shape, F32)],
        compiler_params=pltpu.CompilerParams(vmem_limit_bytes=VMEM_BYTES),
        name="side_maps",
    )(place, own, *received)


def emit_kernel(group, place, before, own, one, two, three, z, y, gate, gain, out, slots, state):
    me = place[0]

    @pl.when(pl.program_id(0) == 0)
    def enter():
        for d, got in enumerate((own, one, two, three)):
            slots[d] = got[...]
        for h in range(2):
            s = jnp.zeros((BLK, BLK), F32)
            for j in range(3):
                at = (me + 4 - j) % 4
                moved = slots[at, h, :, BLK:].astype(F32)
                if j > 0:
                    moved = moved + compose(slots[at, h, :, :BLK].astype(F32), s)
                s = jnp.where(j < me, moved, s)
            s = compose(before[h, :, :BLK], s) + before[h, :, BLK:]
            state[h] = s.astype(BF)

    for j in range(group):
        at = slice(j * BLK, (j + 1) * BLK)
        for h in range(2):
            lanes = slice(h * BLK, (h + 1) * BLK)
            a = y[at, lanes] + dot(z[at, lanes], state[h])
            scale = lax.rsqrt(jnp.mean(a * a, axis=-1, keepdims=True) + GUARD)
            a = a * scale * gain[...] * jax.nn.sigmoid(gate[at, lanes].astype(F32))
            out[at, lanes] = a.astype(BF)


def emit(place, before, own, received, z, y, gate, gain, group=4):
    small = pl.BlockSpec(own.shape, lambda i: (0, 0, 0))
    tall = pl.BlockSpec((group * BLK, 2 * BLK), lambda i: (i, 0))
    return pl.pallas_call(
        functools.partial(emit_kernel, group),
        grid=(z.shape[0] // (group * BLK),),
        in_specs=[pl.BlockSpec(memory_space=pltpu.SMEM)]
        + [small] * 5
        + [tall] * 3
        + [pl.BlockSpec((1, BLK), lambda i: (0, 0))],
        out_specs=tall,
        out_shape=jax.ShapeDtypeStruct(z.shape, BF),
        scratch_shapes=[pltpu.VMEM((4,) + own.shape, BF), pltpu.VMEM((2, BLK, BLK), BF)],
        compiler_params=pltpu.CompilerParams(vmem_limit_bytes=VMEM_BYTES),
        name="emit",
    )(place, before, own, *received, z, y, gate, gain)


def output_kernel(info, a, w, mine, theirs, total):
    core = info[0]
    parts, levels, rows, width = w.shape
    depth = parts * rows
    for i in range(levels):
        more = dot(a[info[1 + i]], w[:, i].reshape(depth, width))
        total[...] = more if i == 0 else total[...] + more
    mine[...] = total[pl.ds(pl.multiple_of(core * BLK, BLK), BLK), :]
    theirs[...] = total[pl.ds(pl.multiple_of((1 - core) * BLK, BLK), BLK), :].astype(BF)


def fetch_kernel(far, near, sem):
    copy = pltpu.make_async_copy(far, near, sem)
    copy.start()
    copy.wait()


def fetched(array):
    return pl.pallas_call(
        fetch_kernel,
        in_specs=[pl.BlockSpec(memory_space=pl.ANY)],
        out_specs=pl.BlockSpec(memory_space=pltpu.VMEM),
        out_shape=jax.ShapeDtypeStruct(array.shape, array.dtype),
        scratch_shapes=[pltpu.SemaphoreType.DMA(())],
        compiler_params=pltpu.CompilerParams(vmem_limit_bytes=16 * 1024 * 1024),
        cost_estimate=pl.CostEstimate(
            flops=10 * 10**9, bytes_accessed=4 * array.size, transcendentals=0
        ),
        name="fetched",
    )(array)


def output_rows(info, normed, weight):
    parts, levels, rows, width = weight.shape
    here = pl.BlockSpec(memory_space=pltpu.VMEM)
    return pl.pallas_call(
        output_kernel,
        in_specs=[pl.BlockSpec(memory_space=pltpu.SMEM), here, here],
        out_specs=[here, here],
        scratch_shapes=[
            pltpu.VMEM((2 * BLK, width), F32),
        ],
        out_shape=[
            jax.ShapeDtypeStruct((BLK, width), F32),
            jax.ShapeDtypeStruct((BLK, width), BF),
        ],
        compiler_params=pltpu.CompilerParams(vmem_limit_bytes=VMEM_BYTES),
        cost_estimate=pl.CostEstimate(
            flops=4 * BLK * parts * levels * rows * width,
            bytes_accessed=2 * parts * levels * rows * width,
            transcendentals=0,
        ),
        name="output_rows",
    )(info, normed, weight)


def turn(array, axis, pairs):
    return lax.ppermute(array, axis, pairs)


def along_y(d):
    return [(4 * x + y, 4 * x + (y + d) % 4) for x in range(4) for y in range(4)]


def along_x(d):
    return [(4 * x + y, 4 * ((x + d) % 4) + y) for x in range(4) for y in range(4)]


def across():
    return [(t, t ^ 1) for t in range(16)]


def along_z(d):
    return [(2 * z + k, 2 * ((z + d) % 8) + k) for z in range(8) for k in range(2)]


def after(array, *others):
    return lax.optimization_barrier((array,) + others)[0]


SAME_CORE = [[2 * z + k for z in range(8)] for k in range(2)]


def latent_rows(tokens, kv_weight, kv_gain):
    latent = dot(tokens, kv_weight)
    scale = lax.rsqrt(jnp.mean(latent * latent, axis=-1, keepdims=True) + GUARD)
    return (latent * scale * kv_gain).astype(BF)


def pick_kernel(info, tile, out):
    out[...] = jnp.where(info[4 + pl.program_id(0)] > 0, tile[...], jnp.zeros_like(out))


def picked(tiles, owner, ctx):
    owners = owner.reshape(-1)
    count = owners.shape[0]
    order = jnp.arange(count, dtype=jnp.int32)
    same = owners[:, None] == owners[None, :]
    rank = jnp.sum((same & (order[None, :] < order[:, None])).astype(jnp.int32), axis=1)
    slots = jnp.arange(4, dtype=jnp.int32)[:, None]
    wanted = ((owners[None, :] == ctx) & (rank[None, :] == slots)).astype(jnp.int32)
    source = jnp.sum(wanted * order[None, :], axis=1)
    place = 4 * ((ctx // 4 - source // 4 + 4) % 4) + (ctx % 4 - source % 4 + 4) % 4
    info = jnp.concatenate([place, jnp.sum(wanted, axis=1)]).astype(jnp.int32)
    shape = tiles.shape[1:]
    return pl.pallas_call(
        pick_kernel,
        grid_spec=pltpu.PrefetchScalarGridSpec(
            num_scalar_prefetch=1,
            grid=(4,),
            in_specs=[pl.BlockSpec((1,) + shape, lambda i, info: (info[i], 0, 0))],
            out_specs=pl.BlockSpec((1,) + shape, lambda i, info: (i, 0, 0)),
        ),
        out_shape=jax.ShapeDtypeStruct((4,) + shape, tiles.dtype),
        compiler_params=pltpu.CompilerParams(vmem_limit_bytes=VMEM_BYTES),
        name="picked",
    )(info, tiles)


def body(
    tokens,
    query_weight,
    key_weight,
    values_projector_matrix,
    gate_weight,
    beta_weight,
    beta_bias,
    log_decay,
    head_gain,
    output_weight,
    kv_weight,
    kv_gain,
    owner,
):
    ctx = lax.axis_index("ctx").astype(jnp.int32)
    tp = lax.axis_index("tp").astype(jnp.int32)
    level, core = tp // 2, tp % 2
    spare = BLK - beta_weight.shape[1]

    gathered = lax.all_gather(tokens, "tp", axis=0, tiled=True)
    rate_weight = jnp.pad(beta_weight, ((0, 0), (0, spare)))
    bias = jnp.pad(beta_bias, (0, spare))[None]
    latent = latent_rows(tokens, kv_weight, kv_gain)
    tiles = jnp.stack([latent] + [turn(latent, "ctx", along_y(d)) for d in (1, 2, 3)])
    tiles = jnp.concatenate([tiles] + [turn(tiles, "ctx", along_x(d)) for d in (1, 2, 3)])
    cache = picked(tiles, owner, ctx)

    part = lax.dynamic_slice_in_dim(output_weight, ctx * 16, 16, 0)
    up, down = [part], [part]
    for s in range(4):
        up.append(turn(up[-1], "tp", along_z(1)))
        if s < 3:
            down.append(turn(down[-1], "tp", along_z(-1)))
    part = jnp.concatenate(up + down[:0:-1], axis=0)
    gathered = after(gathered, cache, part, rate_weight)
    all_parts = lax.all_gather(part, "ctx", axis=0, tiled=True)
    all_parts = all_parts.reshape(16, 8, 16, output_weight.shape[1])

    fallen, solved, states, maps, low = delta_blocks(
        gathered, log_decay, key_weight, values_projector_matrix, rate_weight, bias
    )
    z, y = rise(dot(gathered, query_weight), log_decay, fallen, solved, states)
    two, one, three = [turn(low, "ctx", along_y(d)) for d in (2, 1, 3)]
    before, total = side_maps((ctx % 4)[None], maps, (one, two, three))
    two, one, three = [turn(total, "ctx", along_x(d)) for d in (2, 1, 3)]
    gate = dot(gathered, gate_weight).astype(BF)
    normed = emit((ctx // 4)[None], before, total, (one, two, three), z, y, gate, head_gain[None])

    normed = lax.all_to_all(
        normed.reshape(8, 2 * BLK, 2 * BLK), "tp", 0, 0, tiled=True, axis_index_groups=SAME_CORE
    )
    info = jnp.stack([core] + [(level + 8 - i) % 8 for i in range(8)])
    mine, theirs = output_rows(info, normed, fetched(all_parts))
    theirs = turn(theirs, "tp", across())
    return (mine + theirs.astype(F32)).astype(BF), cache


def solution(mesh):
    in_specs = (
        P(("ctx", "tp"), None),
        P(None, "tp"),
        P(None, "tp"),
        P(None, "tp"),
        P(None, "tp"),
        P(None, "tp"),
        P("tp"),
        P("ctx", "tp"),
        P(),
        P("tp", None),
        P(),
        P(),
        P(None, "tp"),
    )
    out_specs = (P(("ctx", "tp"), None), P("ctx", "tp", None))
    return jax.shard_map(body, mesh=mesh, in_specs=in_specs, out_specs=out_specs, check_vma=False)
```

```python
import functools
import jax
import jax.numpy as jnp
from jax import lax
from jax.experimental import pallas as pl
from jax.experimental.pallas import tpu as pltpu
from jax.sharding import PartitionSpec as P

BLK = 128
GUARD = 1e-06
BF = jnp.bfloat16
F32 = jnp.float32
VMEM_BYTES = 24 * 1024 * 1024


def dot(a, b, contract=((1,), (0,))):
    return lax.dot_general(a, b, (contract, ((), ())), preferred_element_type=F32)


def halves(a):
    high = a.astype(BF)
    return high, (a - high.astype(F32)).astype(BF)


def wide_left(a):
    return jnp.concatenate(halves(a), axis=1)


def wide_right(b):
    row = jnp.concatenate(halves(b), axis=1)
    return jnp.concatenate([row, row], axis=0)


def wide_dot(left, right):
    both = dot(left, right)
    n = both.shape[1] // 2
    return both[:, :n] + both[:, n:]


def indices(shape):
    return lax.broadcasted_iota(jnp.int32, shape, 0), lax.broadcasted_iota(jnp.int32, shape, 1)


def inverses(systems, row, col):
    eye = (row == col).astype(F32)
    joins = (row // 2 == col // 2) & (row > col)
    out = [eye - jnp.where(joins, s, 0.0) for s in systems]
    size = 2
    while size < BLK:
        joins = (row // (2 * size) == col // (2 * size)) & (row // size > col // size)
        parts = [jnp.where(joins, s, 0.0) for s in systems]
        lefts = [wide_left(t) for t in out]
        rights = [wide_right(t) for t in out]
        inner = [wide_dot(wide_left(p), r) for p, r in zip(parts, rights)]
        out = [t - wide_dot(l, wide_right(x)) for t, l, x in zip(out, lefts, inner)]
        size *= 2
    return out


def running(decay, ones):
    high = decay.astype(BF)
    rest = decay - high.astype(F32)
    mid = rest.astype(BF)
    low = (rest - mid.astype(F32)).astype(BF)
    both = dot(jnp.concatenate([ones, ones], axis=1), jnp.concatenate([high, mid], axis=0))
    return both + dot(ones, low)


def unit(rows):
    return rows * lax.rsqrt(jnp.sum(rows * rows, axis=-1, keepdims=True) + GUARD)


def delta_kernel(
    group, proj, ld, bias, k_out, w_out, s_out, x_out, low_out, rate, held
):
    first = pl.program_id(0) == 0
    lanes2 = 2 * BLK
    rate[...] = jax.nn.sigmoid(proj[:, 2 * lanes2 :] + bias[...])

    @pl.when(first)
    def start():
        across, along = indices((BLK, lanes2))
        for h in range(2):
            held[h] = (across == along).astype(F32)

    row, col = indices((BLK, BLK))
    ones = (row >= col).astype(BF)
    pairs = []
    for blk in range(group):
        at = slice(blk * BLK, (blk + 1) * BLK)
        decay = ld[at, :]
        cum = running(decay, ones)
        for h in range(2):
            lanes = slice(h * BLK, (h + 1) * BLK)
            pairs.append((blk, at, h, lanes, cum[:, lanes]))
    systems, targets, ends, finals = [], [], [], []
    for blk, at, h, lanes, c in pairs:
        k = unit(proj[at, lanes])
        v = proj[at, lanes2 + h * BLK : lanes2 + (h + 1) * BLK]
        beta = rate[at, h : h + 1]
        final = c[BLK - 1 : BLK, :]
        grow = jnp.exp(c)
        k_up = k * grow
        k_down = (k * jnp.exp(-c)).astype(BF)
        k_end = k * jnp.exp(final - c)
        k_out[at, lanes] = k_down
        gram = dot(k_up.astype(BF), k_down, ((1,), (1,)))
        systems.append(jnp.where(row > col, beta * gram, 0.0))
        targets.append(jnp.concatenate([(beta * k_up).astype(BF), (beta * v).astype(BF)], axis=1))
        ends.append(k_end.T.astype(BF))
        finals.append(jnp.exp(final))
    solved = inverses(systems, row, col)
    solved = [dot(t.astype(BF), g).astype(BF) for t, g in zip(solved, targets)]
    maps = {}
    for (blk, at, h, lanes, c), w_, e, last in zip(pairs, solved, ends, finals):
        w_out[blk, h] = w_
        both = dot(e, w_)
        m, n = jnp.where(row == col, last, 0.0) - both[:, :BLK], both[:, BLK:]
        maps[blk, h] = m, n
    joint = {}
    for pair in range(group // 2):
        for h in range(2):
            joint[pair, h] = follow(maps[2 * pair + 1, h], jnp.concatenate(maps[2 * pair, h], axis=1))
    x = [held[h] for h in range(2)]
    for pair in range(group // 2):
        for h in range(2):
            s_out[2 * pair, h] = x[h].astype(BF)
            s_out[2 * pair + 1, h] = follow(maps[2 * pair, h], x[h]).astype(BF)
            m, n = joint[pair, h][:, :BLK], joint[pair, h][:, BLK:]
            x[h] = follow((m, n), x[h])
    for h in range(2):
        held[h] = x[h]
        x_out[h] = x[h]
        low_out[h] = x[h].astype(BF)


def narrow_left(a):
    high, low = halves(a)
    return jnp.concatenate([high, low], axis=1), high


def compose(a, x):
    left, high = narrow_left(a)
    x_high, x_low = halves(x)
    return dot(left, jnp.concatenate([x_high, x_high], axis=0)) + dot(high, x_low)


def follow(step, x):
    moved = compose(step[0], x)
    return jnp.concatenate([moved[:, :BLK], moved[:, BLK:] + step[1]], axis=1)


def delta_blocks(projected, ld, bias, group=4):
    rows, width = projected.shape
    blocks = rows // BLK
    lanes = 2 * BLK
    tall = pl.BlockSpec((group * BLK, lanes), lambda i: (i, 0))
    square = pl.BlockSpec((group, 2, BLK, lanes), lambda i: (i, 0, 0, 0))
    last = pl.BlockSpec((2, BLK, lanes), lambda i: (0, 0, 0))
    return pl.pallas_call(
        functools.partial(delta_kernel, group),
        grid=(blocks // group,),
        in_specs=[
            pl.BlockSpec((group * BLK, width), lambda i: (i, 0)),
            tall,
            pl.BlockSpec(bias.shape, lambda i: (0, 0)),
        ],
        out_specs=[tall, square, square, last, last],
        out_shape=[
            jax.ShapeDtypeStruct((rows, lanes), BF),
            jax.ShapeDtypeStruct((blocks, 2, BLK, lanes), BF),
            jax.ShapeDtypeStruct((blocks, 2, BLK, lanes), BF),
            jax.ShapeDtypeStruct((2, BLK, lanes), F32),
            jax.ShapeDtypeStruct((2, BLK, lanes), BF),
        ],
        scratch_shapes=[
            pltpu.VMEM((group * BLK, BLK), F32),
            pltpu.VMEM((2, BLK, lanes), F32),
        ],
        compiler_params=pltpu.CompilerParams(vmem_limit_bytes=VMEM_BYTES),
        cost_estimate=pl.CostEstimate(
            flops=rows * 12 * 10**6, bytes_accessed=rows * 12000, transcendentals=0
        ),
        name="delta_blocks",
    )(projected, ld, bias)


def rise_kernel(group, q, ld, k, w, s, z_out, y_out):
    row, col = indices((BLK, BLK))
    ones = (row >= col).astype(BF)
    todo = [(j, h) for j in range(group) for h in range(2)]
    places = [(slice(j * BLK, (j + 1) * BLK), slice(h * BLK, (h + 1) * BLK)) for j, h in todo]
    grow = [jnp.exp(running(ld[j * BLK : (j + 1) * BLK], ones)) for j in range(group)]
    ups = [unit(q[p]) * grow[j][:, p[1]] for p, (j, h) in zip(places, todo)]
    grams = [dot(u.astype(BF), k[p], ((1,), (1,))) for u, p in zip(ups, places)]
    grams = [jnp.where(row >= col, g, 0.0).astype(BF) for g in grams]
    both = [dot(g, w[j, h]) for g, (j, h) in zip(grams, todo)]
    rises = [(u - b[:, :BLK]).astype(BF) for u, b in zip(ups, both)]
    for p, b, r, (j, h) in zip(places, both, rises, todo):
        seen = dot(r, s[j, h])
        z_out[p] = seen[:, :BLK].astype(BF)
        y_out[p] = seen[:, BLK:] + b[:, BLK:]


def rise(q, ld, k, w, s, group=4):
    rows, lanes = q.shape
    tall = pl.BlockSpec((group * BLK, lanes), lambda i: (i, 0))
    square = pl.BlockSpec((group,) + w.shape[1:], lambda i: (i, 0, 0, 0))
    return pl.pallas_call(
        functools.partial(rise_kernel, group),
        grid=(rows // (group * BLK),),
        in_specs=[tall, tall, tall, square, square],
        out_specs=[tall, tall],
        out_shape=[jax.ShapeDtypeStruct((rows, lanes), BF), jax.ShapeDtypeStruct((rows, lanes), F32)],
        compiler_params=pltpu.CompilerParams(vmem_limit_bytes=VMEM_BYTES),
        cost_estimate=pl.CostEstimate(
            flops=rows * 3 * 10**6, bytes_accessed=rows * 6000, transcendentals=0
        ),
        name="rise",
    )(q, ld, k, w, s)


def side_kernel(place, own, one, two, three, before, total, slots):
    me = place[0]
    for h in range(2):
        slots[0, h] = own[h]
        for d, got in enumerate((one, two, three)):
            slots[d + 1, h] = got[h].astype(F32)
    row, col = indices((BLK, 2 * BLK))
    maps = [None, None]
    for j in range(4):

        @pl.when(me == j)
        def keep():
            for h in range(2):
                before[h] = (row == col).astype(F32) if j == 0 else maps[h]

        at = (me + 4 - j) % 4
        for h in range(2):
            if j == 0:
                maps[h] = slots[at, h]
            else:
                moved = compose(slots[at, h, :, :BLK], maps[h])
                maps[h] = jnp.concatenate(
                    [moved[:, :BLK], moved[:, BLK:] + slots[at, h, :, BLK:]], axis=1
                )
    for h in range(2):
        total[h] = maps[h].astype(BF)


def side_maps(place, own, received):
    whole = pl.BlockSpec(own.shape, lambda i: (0, 0, 0))
    return pl.pallas_call(
        side_kernel,
        grid=(1,),
        in_specs=[pl.BlockSpec(memory_space=pltpu.SMEM)] + [whole] * 4,
        out_specs=[whole, whole],
        out_shape=[jax.ShapeDtypeStruct(own.shape, F32), jax.ShapeDtypeStruct(own.shape, BF)],
        scratch_shapes=[pltpu.VMEM((4,) + own.shape, F32)],
        compiler_params=pltpu.CompilerParams(vmem_limit_bytes=VMEM_BYTES),
        name="side_maps",
    )(place, own, *received)


def emit_kernel(group, place, before, own, one, two, three, z, y, gate, gain, out, slots, state):
    me = place[0]

    @pl.when(pl.program_id(0) == 0)
    def enter():
        for d, got in enumerate((own, one, two, three)):
            slots[d] = got[...]
        for h in range(2):
            s = jnp.zeros((BLK, BLK), F32)
            for j in range(3):
                at = (me + 4 - j) % 4
                moved = slots[at, h, :, BLK:].astype(F32)
                if j > 0:
                    moved = moved + compose(slots[at, h, :, :BLK].astype(F32), s)
                s = jnp.where(j < me, moved, s)
            s = compose(before[h, :, :BLK], s) + before[h, :, BLK:]
            state[h] = s.astype(BF)

    for j in range(group):
        at = slice(j * BLK, (j + 1) * BLK)
        for h in range(2):
            lanes = slice(h * BLK, (h + 1) * BLK)
            a = y[at, lanes] + dot(z[at, lanes], state[h])
            scale = lax.rsqrt(jnp.mean(a * a, axis=-1, keepdims=True) + GUARD)
            a = a * scale * gain[...] * jax.nn.sigmoid(gate[at, lanes].astype(F32))
            out[at, lanes] = a.astype(BF)


def emit(place, before, own, received, z, y, gate, gain, group=4):
    small = pl.BlockSpec(own.shape, lambda i: (0, 0, 0))
    tall = pl.BlockSpec((group * BLK, 2 * BLK), lambda i: (i, 0))
    return pl.pallas_call(
        functools.partial(emit_kernel, group),
        grid=(z.shape[0] // (group * BLK),),
        in_specs=[pl.BlockSpec(memory_space=pltpu.SMEM)]
        + [small] * 5
        + [tall] * 3
        + [pl.BlockSpec((1, BLK), lambda i: (0, 0))],
        out_specs=tall,
        out_shape=jax.ShapeDtypeStruct(z.shape, BF),
        scratch_shapes=[pltpu.VMEM((4,) + own.shape, BF), pltpu.VMEM((2, BLK, BLK), BF)],
        compiler_params=pltpu.CompilerParams(vmem_limit_bytes=VMEM_BYTES),
        name="emit",
    )(place, before, own, *received, z, y, gate, gain)


def output_kernel(info, a, w, mine, theirs, total):
    core = info[0]
    parts, levels, rows, width = w.shape
    depth = parts * rows
    for i in range(levels):
        more = dot(a[info[1 + i]], w[:, i].reshape(depth, width))
        total[...] = more if i == 0 else total[...] + more
    mine[...] = total[pl.ds(pl.multiple_of(core * BLK, BLK), BLK), :]
    theirs[...] = total[pl.ds(pl.multiple_of((1 - core) * BLK, BLK), BLK), :].astype(BF)


def output_rows(info, normed, weight):
    parts, levels, rows, width = weight.shape
    here = pl.BlockSpec(memory_space=pltpu.VMEM)
    return pl.pallas_call(
        output_kernel,
        in_specs=[pl.BlockSpec(memory_space=pltpu.SMEM), here, here],
        out_specs=[here, here],
        scratch_shapes=[
            pltpu.VMEM((2 * BLK, width), F32),
        ],
        out_shape=[
            jax.ShapeDtypeStruct((BLK, width), F32),
            jax.ShapeDtypeStruct((BLK, width), BF),
        ],
        compiler_params=pltpu.CompilerParams(vmem_limit_bytes=VMEM_BYTES),
        cost_estimate=pl.CostEstimate(
            flops=4 * BLK * parts * levels * rows * width,
            bytes_accessed=2 * parts * levels * rows * width,
            transcendentals=0,
        ),
        name="output_rows",
    )(info, normed, weight)


def turn(array, axis, pairs):
    return lax.ppermute(array, axis, pairs)


def along_y(d):
    return [(4 * x + y, 4 * x + (y + d) % 4) for x in range(4) for y in range(4)]


def down_x(d):
    return [(4 * x + y, 4 * (x + d) + y) for x in range(4 - d) for y in range(4)]


def along_x(d):
    return [(4 * x + y, 4 * ((x + d) % 4) + y) for x in range(4) for y in range(4)]


def across():
    return [(t, t ^ 1) for t in range(16)]


def along_z(d):
    return [(2 * z + k, 2 * ((z + d) % 8) + k) for z in range(8) for k in range(2)]


def after(array, *others):
    return lax.optimization_barrier((array,) + others)[0]


SAME_CORE = [[2 * z + k for z in range(8)] for k in range(2)]


def latent_rows(tokens, kv_weight, kv_gain):
    latent = dot(tokens, kv_weight)
    scale = lax.rsqrt(jnp.mean(latent * latent, axis=-1, keepdims=True) + GUARD)
    return (latent * scale * kv_gain).astype(BF)


def pick_kernel(info, tile, out):
    out[...] = jnp.where(info[4 + pl.program_id(0)] > 0, tile[...], jnp.zeros_like(out))


def picked(tiles, owner, ctx):
    owners = owner.reshape(-1)
    count = owners.shape[0]
    order = jnp.arange(count, dtype=jnp.int32)
    same = owners[:, None] == owners[None, :]
    rank = jnp.sum((same & (order[None, :] < order[:, None])).astype(jnp.int32), axis=1)
    slots = jnp.arange(4, dtype=jnp.int32)[:, None]
    wanted = ((owners[None, :] == ctx) & (rank[None, :] == slots)).astype(jnp.int32)
    source = jnp.sum(wanted * order[None, :], axis=1)
    place = 4 * ((ctx // 4 - source // 4 + 4) % 4) + (ctx % 4 - source % 4 + 4) % 4
    info = jnp.concatenate([place, jnp.sum(wanted, axis=1)]).astype(jnp.int32)
    shape = tiles.shape[1:]
    return pl.pallas_call(
        pick_kernel,
        grid_spec=pltpu.PrefetchScalarGridSpec(
            num_scalar_prefetch=1,
            grid=(4,),
            in_specs=[pl.BlockSpec((1,) + shape, lambda i, info: (info[i], 0, 0))],
            out_specs=pl.BlockSpec((1,) + shape, lambda i, info: (i, 0, 0)),
        ),
        out_shape=jax.ShapeDtypeStruct((4,) + shape, tiles.dtype),
        compiler_params=pltpu.CompilerParams(vmem_limit_bytes=VMEM_BYTES),
        name="picked",
    )(info, tiles)


def body(
    tokens,
    query_weight,
    key_weight,
    values_projector_matrix,
    gate_weight,
    beta_weight,
    beta_bias,
    log_decay,
    head_gain,
    output_weight,
    kv_weight,
    kv_gain,
    owner,
):
    ctx = lax.axis_index("ctx").astype(jnp.int32)
    tp = lax.axis_index("tp").astype(jnp.int32)
    level, core = tp // 2, tp % 2
    spare = BLK - beta_weight.shape[1]

    gathered = lax.all_gather(tokens, "tp", axis=0, tiled=True)
    rate_weight = jnp.pad(beta_weight, ((0, 0), (0, spare)))
    weights = jnp.concatenate([key_weight, values_projector_matrix, rate_weight], axis=1)
    bias = jnp.pad(beta_bias, (0, spare))[None]
    latent = latent_rows(tokens, kv_weight, kv_gain)
    tiles = jnp.stack([latent] + [turn(latent, "ctx", along_y(d)) for d in (1, 2, 3)])
    tiles = jnp.concatenate([tiles] + [turn(tiles, "ctx", along_x(d)) for d in (1, 2, 3)])
    cache = picked(tiles, owner, ctx)

    part = lax.dynamic_slice_in_dim(output_weight, ctx * 16, 16, 0)
    up, down = [part], [part]
    for s in range(4):
        up.append(turn(up[-1], "tp", along_z(1)))
        if s < 3:
            down.append(turn(down[-1], "tp", along_z(-1)))
    part = jnp.concatenate(up + down[:0:-1], axis=0)
    gathered = after(gathered, cache, part, weights)
    all_parts = lax.all_gather(part, "ctx", axis=0, tiled=True)
    all_parts = all_parts.reshape(16, 8, 16, output_weight.shape[1])

    fallen, solved, states, maps, low = delta_blocks(dot(gathered, weights), log_decay, bias)
    z, y = rise(dot(gathered, query_weight), log_decay, fallen, solved, states)
    two, one, three = [turn(low, "ctx", along_y(d)) for d in (2, 1, 3)]
    before, total = side_maps((ctx % 4)[None], maps, (one, two, three))
    two, one, three = [turn(total, "ctx", down_x(d)) for d in (2, 1, 3)]
    gate = dot(gathered, gate_weight).astype(BF)
    normed = emit((ctx // 4)[None], before, total, (one, two, three), z, y, gate, head_gain[None])

    normed = lax.all_to_all(
        normed.reshape(8, 2 * BLK, 2 * BLK), "tp", 0, 0, tiled=True, axis_index_groups=SAME_CORE
    )
    info = jnp.stack([core] + [(level + 8 - i) % 8 for i in range(8)])
    mine, theirs = output_rows(info, normed, all_parts)
    theirs = turn(theirs, "tp", across())
    return (mine + theirs.astype(F32)).astype(BF), cache


def solution(mesh):
    in_specs = (
        P(("ctx", "tp"), None),
        P(None, "tp"),
        P(None, "tp"),
        P(None, "tp"),
        P(None, "tp"),
        P(None, "tp"),
        P("tp"),
        P("ctx", "tp"),
        P(),
        P("tp", None),
        P(),
        P(),
        P(None, "tp"),
    )
    out_specs = (P(("ctx", "tp"), None), P("ctx", "tp", None))
    return jax.shard_map(body, mesh=mesh, in_specs=in_specs, out_specs=out_specs, check_vma=False)
```

```python
import functools
import jax
import jax.numpy as jnp
from jax import lax
from jax.experimental import pallas as pl
from jax.experimental.pallas import tpu as pltpu
from jax.sharding import PartitionSpec as P

BLK = 128
GUARD = 1e-06
BF = jnp.bfloat16
F32 = jnp.float32
VMEM_BYTES = 24 * 1024 * 1024


def dot(a, b, contract=((1,), (0,))):
    return lax.dot_general(a, b, (contract, ((), ())), preferred_element_type=F32)


def halves(a):
    high = a.astype(BF)
    return high, (a - high.astype(F32)).astype(BF)


def wide_left(a):
    return jnp.concatenate(halves(a), axis=1)


def wide_right(b):
    row = jnp.concatenate(halves(b), axis=1)
    return jnp.concatenate([row, row], axis=0)


def wide_dot(left, right):
    both = dot(left, right)
    n = both.shape[1] // 2
    return both[:, :n] + both[:, n:]


def indices(shape):
    return lax.broadcasted_iota(jnp.int32, shape, 0), lax.broadcasted_iota(jnp.int32, shape, 1)


def inverses(systems, row, col):
    eye = (row == col).astype(F32)
    joins = (row // 2 == col // 2) & (row > col)
    out = [eye - jnp.where(joins, s, 0.0) for s in systems]
    size = 2
    while size < BLK:
        joins = (row // (2 * size) == col // (2 * size)) & (row // size > col // size)
        parts = [jnp.where(joins, s, 0.0) for s in systems]
        lefts = [wide_left(t) for t in out]
        rights = [wide_right(t) for t in out]
        inner = [wide_dot(wide_left(p), r) for p, r in zip(parts, rights)]
        out = [t - wide_dot(l, wide_right(x)) for t, l, x in zip(out, lefts, inner)]
        size *= 2
    return out


def running(decay, ones):
    high = decay.astype(BF)
    rest = decay - high.astype(F32)
    mid = rest.astype(BF)
    low = (rest - mid.astype(F32)).astype(BF)
    both = dot(jnp.concatenate([ones, ones], axis=1), jnp.concatenate([high, mid], axis=0))
    return both + dot(ones, low)


def unit(rows):
    return rows * lax.rsqrt(jnp.sum(rows * rows, axis=-1, keepdims=True) + GUARD)


def delta_kernel(
    group, proj, ld, bias, k_out, w_out, s_out, x_out, low_out, rate, held
):
    first = pl.program_id(0) == 0
    lanes2 = 2 * BLK
    rate[...] = jax.nn.sigmoid(proj[:, 2 * lanes2 :] + bias[...])

    @pl.when(first)
    def start():
        across, along = indices((BLK, lanes2))
        for h in range(2):
            held[h] = (across == along).astype(F32)

    row, col = indices((BLK, BLK))
    ones = (row >= col).astype(BF)
    pairs = []
    for blk in range(group):
        at = slice(blk * BLK, (blk + 1) * BLK)
        decay = ld[at, :]
        cum = running(decay, ones)
        for h in range(2):
            lanes = slice(h * BLK, (h + 1) * BLK)
            pairs.append((blk, at, h, lanes, cum[:, lanes]))
    systems, targets, ends, finals = [], [], [], []
    for blk, at, h, lanes, c in pairs:
        k = unit(proj[at, lanes])
        v = proj[at, lanes2 + h * BLK : lanes2 + (h + 1) * BLK]
        beta = rate[at, h : h + 1]
        final = c[BLK - 1 : BLK, :]
        grow = jnp.exp(c)
        k_up = k * grow
        k_down = (k * jnp.exp(-c)).astype(BF)
        k_end = k * jnp.exp(final - c)
        k_out[at, lanes] = k_down
        gram = dot(k_up.astype(BF), k_down, ((1,), (1,)))
        systems.append(jnp.where(row > col, beta * gram, 0.0))
        targets.append(jnp.concatenate([(beta * k_up).astype(BF), (beta * v).astype(BF)], axis=1))
        ends.append(k_end.T.astype(BF))
        finals.append(jnp.exp(final))
    solved = inverses(systems, row, col)
    solved = [dot(t.astype(BF), g).astype(BF) for t, g in zip(solved, targets)]
    maps = {}
    for (blk, at, h, lanes, c), w_, e, last in zip(pairs, solved, ends, finals):
        w_out[blk, h] = w_
        both = dot(e, w_)
        m, n = jnp.where(row == col, last, 0.0) - both[:, :BLK], both[:, BLK:]
        maps[blk, h] = m, n
    joint = {}
    for pair in range(group // 2):
        for h in range(2):
            joint[pair, h] = follow(maps[2 * pair + 1, h], jnp.concatenate(maps[2 * pair, h], axis=1))
    x = [held[h] for h in range(2)]
    for pair in range(group // 2):
        for h in range(2):
            s_out[2 * pair, h] = x[h].astype(BF)
            s_out[2 * pair + 1, h] = follow(maps[2 * pair, h], x[h]).astype(BF)
            m, n = joint[pair, h][:, :BLK], joint[pair, h][:, BLK:]
            x[h] = follow((m, n), x[h])
    for h in range(2):
        held[h] = x[h]
        x_out[h] = x[h]
        low_out[h] = x[h].astype(BF)


def narrow_left(a):
    high, low = halves(a)
    return jnp.concatenate([high, low], axis=1), high


def compose(a, x):
    left, high = narrow_left(a)
    x_high, x_low = halves(x)
    return dot(left, jnp.concatenate([x_high, x_high], axis=0)) + dot(high, x_low)


def follow(step, x):
    moved = compose(step[0], x)
    return jnp.concatenate([moved[:, :BLK], moved[:, BLK:] + step[1]], axis=1)


def delta_blocks(projected, ld, bias, group=4):
    rows, width = projected.shape
    blocks = rows // BLK
    lanes = 2 * BLK
    tall = pl.BlockSpec((group * BLK, lanes), lambda i: (i, 0))
    square = pl.BlockSpec((group, 2, BLK, lanes), lambda i: (i, 0, 0, 0))
    last = pl.BlockSpec((2, BLK, lanes), lambda i: (0, 0, 0))
    return pl.pallas_call(
        functools.partial(delta_kernel, group),
        grid=(blocks // group,),
        in_specs=[
            pl.BlockSpec((group * BLK, width), lambda i: (i, 0)),
            tall,
            pl.BlockSpec(bias.shape, lambda i: (0, 0)),
        ],
        out_specs=[tall, square, square, last, last],
        out_shape=[
            jax.ShapeDtypeStruct((rows, lanes), BF),
            jax.ShapeDtypeStruct((blocks, 2, BLK, lanes), BF),
            jax.ShapeDtypeStruct((blocks, 2, BLK, lanes), BF),
            jax.ShapeDtypeStruct((2, BLK, lanes), F32),
            jax.ShapeDtypeStruct((2, BLK, lanes), BF),
        ],
        scratch_shapes=[
            pltpu.VMEM((group * BLK, BLK), F32),
            pltpu.VMEM((2, BLK, lanes), F32),
        ],
        compiler_params=pltpu.CompilerParams(vmem_limit_bytes=VMEM_BYTES),
        cost_estimate=pl.CostEstimate(
            flops=rows * 12 * 10**6, bytes_accessed=rows * 12000, transcendentals=0
        ),
        name="delta_blocks",
    )(projected, ld, bias)


def rise_kernel(group, q, ld, k, w, s, z_out, y_out):
    row, col = indices((BLK, BLK))
    ones = (row >= col).astype(BF)
    todo = [(j, h) for j in range(group) for h in range(2)]
    places = [(slice(j * BLK, (j + 1) * BLK), slice(h * BLK, (h + 1) * BLK)) for j, h in todo]
    grow = [jnp.exp(running(ld[j * BLK : (j + 1) * BLK], ones)) for j in range(group)]
    ups = [unit(q[p]) * grow[j][:, p[1]] for p, (j, h) in zip(places, todo)]
    grams = [dot(u.astype(BF), k[p], ((1,), (1,))) for u, p in zip(ups, places)]
    grams = [jnp.where(row >= col, g, 0.0).astype(BF) for g in grams]
    both = [dot(g, w[j, h]) for g, (j, h) in zip(grams, todo)]
    rises = [(u - b[:, :BLK]).astype(BF) for u, b in zip(ups, both)]
    for p, b, r, (j, h) in zip(places, both, rises, todo):
        seen = dot(r, s[j, h])
        z_out[p] = seen[:, :BLK].astype(BF)
        y_out[p] = seen[:, BLK:] + b[:, BLK:]


def rise(q, ld, k, w, s, group=4):
    rows, lanes = q.shape
    tall = pl.BlockSpec((group * BLK, lanes), lambda i: (i, 0))
    square = pl.BlockSpec((group,) + w.shape[1:], lambda i: (i, 0, 0, 0))
    return pl.pallas_call(
        functools.partial(rise_kernel, group),
        grid=(rows // (group * BLK),),
        in_specs=[tall, tall, tall, square, square],
        out_specs=[tall, tall],
        out_shape=[jax.ShapeDtypeStruct((rows, lanes), BF), jax.ShapeDtypeStruct((rows, lanes), F32)],
        compiler_params=pltpu.CompilerParams(vmem_limit_bytes=VMEM_BYTES),
        cost_estimate=pl.CostEstimate(
            flops=rows * 3 * 10**6, bytes_accessed=rows * 6000, transcendentals=0
        ),
        name="rise",
    )(q, ld, k, w, s)


def side_kernel(place, own, one, two, three, before, total, slots):
    me = place[0]
    for h in range(2):
        slots[0, h] = own[h]
        for d, got in enumerate((one, two, three)):
            slots[d + 1, h] = got[h].astype(F32)
    row, col = indices((BLK, 2 * BLK))
    maps = [None, None]
    for j in range(4):

        @pl.when(me == j)
        def keep():
            for h in range(2):
                before[h] = (row == col).astype(F32) if j == 0 else maps[h]

        at = (me + 4 - j) % 4
        for h in range(2):
            if j == 0:
                maps[h] = slots[at, h]
            else:
                moved = compose(slots[at, h, :, :BLK], maps[h])
                maps[h] = jnp.concatenate(
                    [moved[:, :BLK], moved[:, BLK:] + slots[at, h, :, BLK:]], axis=1
                )
    for h in range(2):
        total[h] = maps[h].astype(BF)


def side_maps(place, own, received):
    whole = pl.BlockSpec(own.shape, lambda i: (0, 0, 0))
    return pl.pallas_call(
        side_kernel,
        grid=(1,),
        in_specs=[pl.BlockSpec(memory_space=pltpu.SMEM)] + [whole] * 4,
        out_specs=[whole, whole],
        out_shape=[jax.ShapeDtypeStruct(own.shape, F32), jax.ShapeDtypeStruct(own.shape, BF)],
        scratch_shapes=[pltpu.VMEM((4,) + own.shape, F32)],
        compiler_params=pltpu.CompilerParams(vmem_limit_bytes=VMEM_BYTES),
        name="side_maps",
    )(place, own, *received)


def emit_kernel(together, info, before, own, one, two, three, gain, *refs):
    ins, outs, (slots, state) = refs[: 3 * together], refs[3 * together : -2], refs[-2:]
    me = info[0]

    @pl.when(pl.program_id(0) == 0)
    def enter():
        for d, got in enumerate((own, one, two, three)):
            slots[d] = got[...]
        for h in range(2):
            s = jnp.zeros((BLK, BLK), F32)
            for j in range(3):
                at = (me + 4 - j) % 4
                moved = slots[at, h, :, BLK:].astype(F32)
                if j > 0:
                    moved = moved + compose(slots[at, h, :, :BLK].astype(F32), s)
                s = jnp.where(j < me, moved, s)
            s = compose(before[h, :, :BLK], s) + before[h, :, BLK:]
            state[h] = s.astype(BF)

    made = []
    for z, y, gate in zip(*(ins[j * together : (j + 1) * together] for j in range(3))):
        done = []
        for h in range(2):
            lanes = slice(h * BLK, (h + 1) * BLK)
            a = y[:, lanes] + dot(z[:, lanes], state[h])
            scale = lax.rsqrt(jnp.mean(a * a, axis=-1, keepdims=True) + GUARD)
            a = a * scale * gain[...] * jax.nn.sigmoid(gate[:, lanes].astype(F32))
            done.append(a.astype(BF))
        made.append(jnp.concatenate(done, axis=1))
    for i in range(len(outs) // together):

        @pl.when(pl.program_id(0) == i)
        def put(i=i):
            for j, rows in enumerate(made):
                outs[i * together + j][...] = rows


def emit(info, before, own, received, z, y, gate, gain, levels, together=2):
    rows, lanes = z.shape
    rows //= levels
    small = pl.BlockSpec(own.shape, lambda i, info: (0, 0, 0))
    tall = [
        pl.BlockSpec((rows, lanes), lambda i, info, j=j: (lax.rem(info[1] + together * i + j, levels), 0))
        for j in range(together)
    ]
    return pl.pallas_call(
        functools.partial(emit_kernel, together),
        grid_spec=pltpu.PrefetchScalarGridSpec(
            num_scalar_prefetch=1,
            grid=(levels // together,),
            in_specs=[small] * 5 + [pl.BlockSpec((1, BLK), lambda i, info: (0, 0))] + tall * 3,
            out_specs=[pl.BlockSpec((rows, lanes), lambda i, info: (0, 0))] * levels,
            scratch_shapes=[pltpu.VMEM((4,) + own.shape, BF), pltpu.VMEM((2, BLK, BLK), BF)],
        ),
        out_shape=[jax.ShapeDtypeStruct((rows, lanes), BF)] * levels,
        compiler_params=pltpu.CompilerParams(vmem_limit_bytes=VMEM_BYTES),
        name="emit",
    )(info, before, own, *received, gain, *[z] * together, *[y] * together, *[gate] * together)


def output_kernel(info, *refs):
    blocks, (w, mine, theirs, total) = refs[:9], refs[9:]
    core = info[0]
    parts, levels, rows, width = w.shape
    depth = parts * rows
    for i in range(levels):
        a = blocks[i][...]
        if i == 4:
            a = jnp.where(core == 0, a, blocks[8][...])
        more = dot(a, w[:, i].reshape(depth, width))
        total[...] = more if i == 0 else total[...] + more
    mine[...] = total[pl.ds(pl.multiple_of(core * BLK, BLK), BLK), :]
    theirs[...] = total[pl.ds(pl.multiple_of((1 - core) * BLK, BLK), BLK), :].astype(BF)


def output_rows(info, blocks, weight):
    parts, levels, rows, width = weight.shape
    here = pl.BlockSpec(memory_space=pltpu.VMEM)
    return pl.pallas_call(
        output_kernel,
        in_specs=[pl.BlockSpec(memory_space=pltpu.SMEM), here] + [here] * len(blocks),
        out_specs=[here, here],
        scratch_shapes=[
            pltpu.VMEM((2 * BLK, width), F32),
        ],
        out_shape=[
            jax.ShapeDtypeStruct((BLK, width), F32),
            jax.ShapeDtypeStruct((BLK, width), BF),
        ],
        compiler_params=pltpu.CompilerParams(vmem_limit_bytes=VMEM_BYTES),
        cost_estimate=pl.CostEstimate(
            flops=4 * BLK * parts * levels * rows * width,
            bytes_accessed=2 * parts * levels * rows * width,
            transcendentals=0,
        ),
        name="output_rows",
    )(info, *blocks, weight)


def turn(array, axis, pairs):
    return lax.ppermute(array, axis, pairs)


def along_y(d):
    return [(4 * x + y, 4 * x + (y + d) % 4) for x in range(4) for y in range(4)]


def down_x(d):
    return [(4 * x + y, 4 * (x + d) + y) for x in range(4 - d) for y in range(4)]


def along_x(d):
    return [(4 * x + y, 4 * ((x + d) % 4) + y) for x in range(4) for y in range(4)]


def across():
    return [(t, t ^ 1) for t in range(16)]


def along_z(d):
    return [(2 * z + k, 2 * ((z + d) % 8) + k) for z in range(8) for k in range(2)]


def after(array, *others):
    return lax.optimization_barrier((array,) + others)[0]


def half_way():
    return [(2 * z + k, 2 * ((z + 4 - 6 * k + 8) % 8) + k) for z in range(8) for k in range(2)]


def rest_of_way():
    return [(2 * z + 1, 2 * ((z + 6) % 8) + 1) for z in range(8)]


def latent_rows(tokens, kv_weight, kv_gain):
    latent = dot(tokens, kv_weight)
    scale = lax.rsqrt(jnp.mean(latent * latent, axis=-1, keepdims=True) + GUARD)
    return (latent * scale * kv_gain).astype(BF)


def pick_kernel(info, tile, out):
    out[...] = jnp.where(info[4 + pl.program_id(0)] > 0, tile[...], jnp.zeros_like(out))


def picked(tiles, owner, ctx):
    owners = owner.reshape(-1)
    count = owners.shape[0]
    order = jnp.arange(count, dtype=jnp.int32)
    same = owners[:, None] == owners[None, :]
    rank = jnp.sum((same & (order[None, :] < order[:, None])).astype(jnp.int32), axis=1)
    slots = jnp.arange(4, dtype=jnp.int32)[:, None]
    wanted = ((owners[None, :] == ctx) & (rank[None, :] == slots)).astype(jnp.int32)
    source = jnp.sum(wanted * order[None, :], axis=1)
    place = 4 * ((ctx // 4 - source // 4 + 4) % 4) + (ctx % 4 - source % 4 + 4) % 4
    info = jnp.concatenate([place, jnp.sum(wanted, axis=1)]).astype(jnp.int32)
    shape = tiles.shape[1:]
    return pl.pallas_call(
        pick_kernel,
        grid_spec=pltpu.PrefetchScalarGridSpec(
            num_scalar_prefetch=1,
            grid=(4,),
            in_specs=[pl.BlockSpec((1,) + shape, lambda i, info: (info[i], 0, 0))],
            out_specs=pl.BlockSpec((1,) + shape, lambda i, info: (i, 0, 0)),
        ),
        out_shape=jax.ShapeDtypeStruct((4,) + shape, tiles.dtype),
        compiler_params=pltpu.CompilerParams(vmem_limit_bytes=VMEM_BYTES),
        name="picked",
    )(info, tiles)


def body(
    tokens,
    query_weight,
    key_weight,
    values_projector_matrix,
    gate_weight,
    beta_weight,
    beta_bias,
    log_decay,
    head_gain,
    output_weight,
    kv_weight,
    kv_gain,
    owner,
):
    ctx = lax.axis_index("ctx").astype(jnp.int32)
    tp = lax.axis_index("tp").astype(jnp.int32)
    level, core = tp // 2, tp % 2
    spare = BLK - beta_weight.shape[1]

    gathered = lax.all_gather(tokens, "tp", axis=0, tiled=True)
    rate_weight = jnp.pad(beta_weight, ((0, 0), (0, spare)))
    weights = jnp.concatenate([key_weight, values_projector_matrix, rate_weight], axis=1)
    bias = jnp.pad(beta_bias, (0, spare))[None]
    latent = latent_rows(tokens, kv_weight, kv_gain)
    tiles = jnp.stack([latent] + [turn(latent, "ctx", along_y(d)) for d in (1, 2, 3)])
    tiles = jnp.concatenate([tiles] + [turn(tiles, "ctx", along_x(d)) for d in (1, 2, 3)])
    cache = picked(tiles, owner, ctx)

    part = lax.dynamic_slice_in_dim(output_weight, ctx * 16, 16, 0)
    up, down = [part], [part]
    for s in range(4):
        up.append(turn(up[-1], "tp", along_z(1)))
        if s < 3:
            down.append(turn(down[-1], "tp", along_z(-1)))
    part = jnp.concatenate(up + down[:0:-1], axis=0)
    gathered = after(gathered, tiles, part, weights)
    all_parts = lax.all_gather(part, "ctx", axis=0, tiled=True)
    all_parts = all_parts.reshape(16, 8, 16, output_weight.shape[1])

    fallen, solved, states, maps, low = delta_blocks(dot(gathered, weights), log_decay, bias)
    z, y = rise(dot(gathered, query_weight), log_decay, fallen, solved, states)
    two, one, three = [turn(low, "ctx", along_y(d)) for d in (2, 1, 3)]
    before, total = side_maps((ctx % 4)[None], maps, (one, two, three))
    two, one, three = [turn(total, "ctx", down_x(d)) for d in (2, 1, 3)]
    gate = dot(gathered, gate_weight).astype(BF)
    info = jnp.stack([ctx // 4, level])
    normed = emit(info, before, total, (one, two, three), z, y, gate, head_gain[None], 8)

    passing = turn(normed[4], "tp", half_way())
    blocks = {0: normed[0], 4: passing}
    for d in (3, 5, 2, 6, 1, 7):
        blocks[d] = turn(normed[d], "tp", along_z(d))
    blocks[8] = turn(passing, "tp", rest_of_way())
    mine, theirs = output_rows(core[None], [blocks[d] for d in range(9)], after(all_parts, cache))
    theirs = turn(theirs, "tp", across())
    return (mine + theirs.astype(F32)).astype(BF), cache


def solution(mesh):
    in_specs = (
        P(("ctx", "tp"), None),
        P(None, "tp"),
        P(None, "tp"),
        P(None, "tp"),
        P(None, "tp"),
        P(None, "tp"),
        P("tp"),
        P("ctx", "tp"),
        P(),
        P("tp", None),
        P(),
        P(),
        P(None, "tp"),
    )
    out_specs = (P(("ctx", "tp"), None), P("ctx", "tp", None))
    return jax.shard_map(body, mesh=mesh, in_specs=in_specs, out_specs=out_specs, check_vma=False)
```

```python
import functools
import jax
import jax.numpy as jnp
from jax import lax
from jax.experimental import pallas as pl
from jax.experimental.pallas import tpu as pltpu
from jax.sharding import PartitionSpec as P

BLK = 128
GUARD = 1e-06
BF = jnp.bfloat16
F32 = jnp.float32
VMEM_BYTES = 24 * 1024 * 1024


def dot(a, b, contract=((1,), (0,))):
    return lax.dot_general(a, b, (contract, ((), ())), preferred_element_type=F32)


def halves(a):
    high = a.astype(BF)
    return high, (a - high.astype(F32)).astype(BF)


def wide_left(a):
    return jnp.concatenate(halves(a), axis=1)


def wide_right(b):
    row = jnp.concatenate(halves(b), axis=1)
    return jnp.concatenate([row, row], axis=0)


def wide_dot(left, right):
    both = dot(left, right)
    n = both.shape[1] // 2
    return both[:, :n] + both[:, n:]


def indices(shape):
    return lax.broadcasted_iota(jnp.int32, shape, 0), lax.broadcasted_iota(jnp.int32, shape, 1)


def inverses(systems, row, col):
    eye = (row == col).astype(F32)
    joins = (row // 2 == col // 2) & (row > col)
    out = [eye - jnp.where(joins, s, 0.0) for s in systems]
    size = 2
    while size < BLK:
        joins = (row // (2 * size) == col // (2 * size)) & (row // size > col // size)
        parts = [jnp.where(joins, s, 0.0) for s in systems]
        lefts = [wide_left(t) for t in out]
        rights = [wide_right(t) for t in out]
        inner = [wide_dot(wide_left(p), r) for p, r in zip(parts, rights)]
        out = [t - wide_dot(l, wide_right(x)) for t, l, x in zip(out, lefts, inner)]
        size *= 2
    return out


def running(decay, ones):
    high = decay.astype(BF)
    rest = decay - high.astype(F32)
    mid = rest.astype(BF)
    low = (rest - mid.astype(F32)).astype(BF)
    both = dot(jnp.concatenate([ones, ones], axis=1), jnp.concatenate([high, mid], axis=0))
    return both + dot(ones, low)


def unit(rows):
    return rows * lax.rsqrt(jnp.sum(rows * rows, axis=-1, keepdims=True) + GUARD)


def delta_kernel(
    group, proj, ld, bias, k_out, w_out, s_out, x_out, low_out, rate, held
):
    first = pl.program_id(0) == 0
    lanes2 = 2 * BLK
    rate[...] = jax.nn.sigmoid(proj[:, 2 * lanes2 :] + bias[...])

    @pl.when(first)
    def start():
        across, along = indices((BLK, lanes2))
        for h in range(2):
            held[h] = (across == along).astype(F32)

    row, col = indices((BLK, BLK))
    ones = (row >= col).astype(BF)
    pairs = []
    for blk in range(group):
        at = slice(blk * BLK, (blk + 1) * BLK)
        decay = ld[at, :]
        cum = running(decay, ones)
        for h in range(2):
            lanes = slice(h * BLK, (h + 1) * BLK)
            pairs.append((blk, at, h, lanes, cum[:, lanes]))
    systems, targets, ends, finals = [], [], [], []
    for blk, at, h, lanes, c in pairs:
        k = unit(proj[at, lanes])
        v = proj[at, lanes2 + h * BLK : lanes2 + (h + 1) * BLK]
        beta = rate[at, h : h + 1]
        final = c[BLK - 1 : BLK, :]
        grow = jnp.exp(c)
        k_up = k * grow
        k_down = (k * jnp.exp(-c)).astype(BF)
        k_end = k * jnp.exp(final - c)
        k_out[at, lanes] = k_down
        gram = dot(k_up.astype(BF), k_down, ((1,), (1,)))
        systems.append(jnp.where(row > col, beta * gram, 0.0))
        targets.append(jnp.concatenate([(beta * k_up).astype(BF), (beta * v).astype(BF)], axis=1))
        ends.append(k_end.T.astype(BF))
        finals.append(jnp.exp(final))
    solved = inverses(systems, row, col)
    solved = [dot(t.astype(BF), g).astype(BF) for t, g in zip(solved, targets)]
    maps = {}
    for (blk, at, h, lanes, c), w_, e, last in zip(pairs, solved, ends, finals):
        w_out[blk, h] = w_
        both = dot(e, w_)
        m, n = jnp.where(row == col, last, 0.0) - both[:, :BLK], both[:, BLK:]
        maps[blk, h] = m, n
    joint = {}
    for pair in range(group // 2):
        for h in range(2):
            joint[pair, h] = follow(maps[2 * pair + 1, h], jnp.concatenate(maps[2 * pair, h], axis=1))
    x = [held[h] for h in range(2)]
    for pair in range(group // 2):
        for h in range(2):
            s_out[2 * pair, h] = x[h].astype(BF)
            s_out[2 * pair + 1, h] = follow(maps[2 * pair, h], x[h]).astype(BF)
            m, n = joint[pair, h][:, :BLK], joint[pair, h][:, BLK:]
            x[h] = follow((m, n), x[h])
    for h in range(2):
        held[h] = x[h]
        x_out[h] = x[h]
        low_out[h] = x[h].astype(BF)


def narrow_left(a):
    high, low = halves(a)
    return jnp.concatenate([high, low], axis=1), high


def compose(a, x):
    left, high = narrow_left(a)
    x_high, x_low = halves(x)
    return dot(left, jnp.concatenate([x_high, x_high], axis=0)) + dot(high, x_low)


def follow(step, x):
    moved = compose(step[0], x)
    return jnp.concatenate([moved[:, :BLK], moved[:, BLK:] + step[1]], axis=1)


def delta_blocks(projected, ld, bias, group=4):
    rows, width = projected.shape
    blocks = rows // BLK
    lanes = 2 * BLK
    tall = pl.BlockSpec((group * BLK, lanes), lambda i: (i, 0))
    square = pl.BlockSpec((group, 2, BLK, lanes), lambda i: (i, 0, 0, 0))
    last = pl.BlockSpec((2, BLK, lanes), lambda i: (0, 0, 0))
    return pl.pallas_call(
        functools.partial(delta_kernel, group),
        grid=(blocks // group,),
        in_specs=[
            pl.BlockSpec((group * BLK, width), lambda i: (i, 0)),
            tall,
            pl.BlockSpec(bias.shape, lambda i: (0, 0)),
        ],
        out_specs=[tall, square, square, last, last],
        out_shape=[
            jax.ShapeDtypeStruct((rows, lanes), BF),
            jax.ShapeDtypeStruct((blocks, 2, BLK, lanes), BF),
            jax.ShapeDtypeStruct((blocks, 2, BLK, lanes), BF),
            jax.ShapeDtypeStruct((2, BLK, lanes), F32),
            jax.ShapeDtypeStruct((2, BLK, lanes), BF),
        ],
        scratch_shapes=[
            pltpu.VMEM((group * BLK, BLK), F32),
            pltpu.VMEM((2, BLK, lanes), F32),
        ],
        compiler_params=pltpu.CompilerParams(vmem_limit_bytes=VMEM_BYTES),
        cost_estimate=pl.CostEstimate(
            flops=rows * 12 * 10**6, bytes_accessed=rows * 12000, transcendentals=0
        ),
        name="delta_blocks",
    )(projected, ld, bias)


def rise_kernel(group, q, ld, k, w, s, z_out, y_out):
    row, col = indices((BLK, BLK))
    ones = (row >= col).astype(BF)
    todo = [(j, h) for j in range(group) for h in range(2)]
    places = [(slice(j * BLK, (j + 1) * BLK), slice(h * BLK, (h + 1) * BLK)) for j, h in todo]
    grow = [jnp.exp(running(ld[j * BLK : (j + 1) * BLK], ones)) for j in range(group)]
    ups = [unit(q[p]) * grow[j][:, p[1]] for p, (j, h) in zip(places, todo)]
    grams = [dot(u.astype(BF), k[p], ((1,), (1,))) for u, p in zip(ups, places)]
    grams = [jnp.where(row >= col, g, 0.0).astype(BF) for g in grams]
    both = [dot(g, w[j, h]) for g, (j, h) in zip(grams, todo)]
    rises = [(u - b[:, :BLK]).astype(BF) for u, b in zip(ups, both)]
    for p, b, r, (j, h) in zip(places, both, rises, todo):
        seen = dot(r, s[j, h])
        z_out[p] = seen[:, :BLK].astype(BF)
        y_out[p] = seen[:, BLK:] + b[:, BLK:]


def rise(q, ld, k, w, s, group=4):
    rows, lanes = q.shape
    tall = pl.BlockSpec((group * BLK, lanes), lambda i: (i, 0))
    square = pl.BlockSpec((group,) + w.shape[1:], lambda i: (i, 0, 0, 0))
    return pl.pallas_call(
        functools.partial(rise_kernel, group),
        grid=(rows // (group * BLK),),
        in_specs=[tall, tall, tall, square, square],
        out_specs=[tall, tall],
        out_shape=[jax.ShapeDtypeStruct((rows, lanes), BF), jax.ShapeDtypeStruct((rows, lanes), F32)],
        compiler_params=pltpu.CompilerParams(vmem_limit_bytes=VMEM_BYTES),
        cost_estimate=pl.CostEstimate(
            flops=rows * 3 * 10**6, bytes_accessed=rows * 6000, transcendentals=0
        ),
        name="rise",
    )(q, ld, k, w, s)


def side_kernel(place, own, one, two, three, before, total, slots):
    me = place[0]
    for h in range(2):
        slots[0, h] = own[h]
        for d, got in enumerate((one, two, three)):
            slots[d + 1, h] = got[h].astype(F32)
    row, col = indices((BLK, 2 * BLK))
    maps = [None, None]
    for j in range(4):

        @pl.when(me == j)
        def keep():
            for h in range(2):
                before[h] = (row == col).astype(F32) if j == 0 else maps[h]

        at = (me + 4 - j) % 4
        for h in range(2):
            if j == 0:
                maps[h] = slots[at, h]
            else:
                moved = compose(slots[at, h, :, :BLK], maps[h])
                maps[h] = jnp.concatenate(
                    [moved[:, :BLK], moved[:, BLK:] + slots[at, h, :, BLK:]], axis=1
                )
    for h in range(2):
        total[h] = maps[h].astype(BF)


def side_maps(place, own, received):
    whole = pl.BlockSpec(own.shape, lambda i: (0, 0, 0))
    return pl.pallas_call(
        side_kernel,
        grid=(1,),
        in_specs=[pl.BlockSpec(memory_space=pltpu.SMEM)] + [whole] * 4,
        out_specs=[whole, whole],
        out_shape=[jax.ShapeDtypeStruct(own.shape, F32), jax.ShapeDtypeStruct(own.shape, BF)],
        scratch_shapes=[pltpu.VMEM((4,) + own.shape, F32)],
        compiler_params=pltpu.CompilerParams(vmem_limit_bytes=VMEM_BYTES),
        name="side_maps",
    )(place, own, *received)


def emit_kernel(together, info, before, own, one, two, three, gain, *refs):
    ins, outs, (slots, state) = refs[: 3 * together], refs[3 * together : -2], refs[-2:]
    me = info[0]

    @pl.when(pl.program_id(0) == 0)
    def enter():
        for d, got in enumerate((own, one, two, three)):
            slots[d] = got[...]
        for h in range(2):
            s = jnp.zeros((BLK, BLK), F32)
            for j in range(3):
                at = (me + 4 - j) % 4
                moved = slots[at, h, :, BLK:].astype(F32)
                if j > 0:
                    moved = moved + compose(slots[at, h, :, :BLK].astype(F32), s)
                s = jnp.where(j < me, moved, s)
            s = compose(before[h, :, :BLK], s) + before[h, :, BLK:]
            state[h] = s.astype(BF)

    made = []
    for z, y, gate in zip(*(ins[j * together : (j + 1) * together] for j in range(3))):
        done = []
        for h in range(2):
            lanes = slice(h * BLK, (h + 1) * BLK)
            a = y[:, lanes] + dot(z[:, lanes], state[h])
            scale = lax.rsqrt(jnp.mean(a * a, axis=-1, keepdims=True) + GUARD)
            a = a * scale * gain[...] * jax.nn.sigmoid(gate[:, lanes].astype(F32))
            done.append(a.astype(BF))
        made.append(jnp.concatenate(done, axis=1))
    for i in range(len(outs) // together):

        @pl.when(pl.program_id(0) == i)
        def put(i=i):
            for j, rows in enumerate(made):
                outs[i * together + j][...] = rows


def emit(info, before, own, received, z, y, gate, gain, levels, together=2):
    rows, lanes = z.shape
    rows //= levels
    small = pl.BlockSpec(own.shape, lambda i, info: (0, 0, 0))
    tall = [
        pl.BlockSpec((rows, lanes), lambda i, info, j=j: (lax.rem(info[1] + together * i + j, levels), 0))
        for j in range(together)
    ]
    return pl.pallas_call(
        functools.partial(emit_kernel, together),
        grid_spec=pltpu.PrefetchScalarGridSpec(
            num_scalar_prefetch=1,
            grid=(levels // together,),
            in_specs=[small] * 5 + [pl.BlockSpec((1, BLK), lambda i, info: (0, 0))] + tall * 3,
            out_specs=[pl.BlockSpec((rows, lanes), lambda i, info: (0, 0))] * levels,
            scratch_shapes=[pltpu.VMEM((4,) + own.shape, BF), pltpu.VMEM((2, BLK, BLK), BF)],
        ),
        out_shape=[jax.ShapeDtypeStruct((rows, lanes), BF)] * levels,
        compiler_params=pltpu.CompilerParams(vmem_limit_bytes=VMEM_BYTES),
        name="emit",
    )(info, before, own, *received, gain, *[z] * together, *[y] * together, *[gate] * together)


ARRIVAL = (0, 4, 3, 5, 2, 6, 8, 1, 7)


def output_kernel(info, *refs):
    blocks, (w, mine, theirs, total) = dict(zip(ARRIVAL, refs[:9])), refs[9:]
    core = info[0]
    parts, levels, rows, width = w.shape
    depth = parts * rows
    for i in range(levels):
        a = blocks[i][...]
        if i == 4:
            a = jnp.where(core == 0, a, blocks[8][...])
        more = dot(a, w[:, i].reshape(depth, width))
        total[...] = more if i == 0 else total[...] + more
    mine[...] = total[pl.ds(pl.multiple_of(core * BLK, BLK), BLK), :]
    theirs[...] = total[pl.ds(pl.multiple_of((1 - core) * BLK, BLK), BLK), :].astype(BF)


def output_rows(info, blocks, weight):
    parts, levels, rows, width = weight.shape
    here = pl.BlockSpec(memory_space=pltpu.VMEM)
    return pl.pallas_call(
        output_kernel,
        in_specs=[pl.BlockSpec(memory_space=pltpu.SMEM), here] + [here] * len(blocks),
        out_specs=[here, here],
        scratch_shapes=[
            pltpu.VMEM((2 * BLK, width), F32),
        ],
        out_shape=[
            jax.ShapeDtypeStruct((BLK, width), F32),
            jax.ShapeDtypeStruct((BLK, width), BF),
        ],
        compiler_params=pltpu.CompilerParams(vmem_limit_bytes=VMEM_BYTES),
        cost_estimate=pl.CostEstimate(
            flops=4 * BLK * parts * levels * rows * width,
            bytes_accessed=2 * parts * levels * rows * width,
            transcendentals=0,
        ),
        name="output_rows",
    )(info, *blocks, weight)


def turn(array, axis, pairs):
    return lax.ppermute(array, axis, pairs)


def along_y(d):
    return [(4 * x + y, 4 * x + (y + d) % 4) for x in range(4) for y in range(4)]


def down_x(d):
    return [(4 * x + y, 4 * (x + d) + y) for x in range(4 - d) for y in range(4)]


def along_x(d):
    return [(4 * x + y, 4 * ((x + d) % 4) + y) for x in range(4) for y in range(4)]


def across():
    return [(t, t ^ 1) for t in range(16)]


def along_z(d):
    return [(2 * z + k, 2 * ((z + d) % 8) + k) for z in range(8) for k in range(2)]


def after(array, *others):
    return lax.optimization_barrier((array,) + others)[0]


def half_way():
    return [(2 * z + k, 2 * ((z + 4 - 6 * k + 8) % 8) + k) for z in range(8) for k in range(2)]


def rest_of_way():
    return [(2 * z + 1, 2 * ((z + 6) % 8) + 1) for z in range(8)]


def latent_rows(tokens, kv_weight, kv_gain):
    latent = dot(tokens, kv_weight)
    scale = lax.rsqrt(jnp.mean(latent * latent, axis=-1, keepdims=True) + GUARD)
    return (latent * scale * kv_gain).astype(BF)


def pick_kernel(info, tile, out):
    out[...] = jnp.where(info[4 + pl.program_id(0)] > 0, tile[...], jnp.zeros_like(out))


def picked(tiles, owner, ctx):
    owners = owner.reshape(-1)
    count = owners.shape[0]
    order = jnp.arange(count, dtype=jnp.int32)
    same = owners[:, None] == owners[None, :]
    rank = jnp.sum((same & (order[None, :] < order[:, None])).astype(jnp.int32), axis=1)
    slots = jnp.arange(4, dtype=jnp.int32)[:, None]
    wanted = ((owners[None, :] == ctx) & (rank[None, :] == slots)).astype(jnp.int32)
    source = jnp.sum(wanted * order[None, :], axis=1)
    place = 4 * ((ctx // 4 - source // 4 + 4) % 4) + (ctx % 4 - source % 4 + 4) % 4
    info = jnp.concatenate([place, jnp.sum(wanted, axis=1)]).astype(jnp.int32)
    shape = tiles.shape[1:]
    return pl.pallas_call(
        pick_kernel,
        grid_spec=pltpu.PrefetchScalarGridSpec(
            num_scalar_prefetch=1,
            grid=(4,),
            in_specs=[pl.BlockSpec((1,) + shape, lambda i, info: (info[i], 0, 0))],
            out_specs=pl.BlockSpec((1,) + shape, lambda i, info: (i, 0, 0)),
        ),
        out_shape=jax.ShapeDtypeStruct((4,) + shape, tiles.dtype),
        compiler_params=pltpu.CompilerParams(vmem_limit_bytes=VMEM_BYTES),
        name="picked",
    )(info, tiles)


def body(
    tokens,
    query_weight,
    key_weight,
    values_projector_matrix,
    gate_weight,
    beta_weight,
    beta_bias,
    log_decay,
    head_gain,
    output_weight,
    kv_weight,
    kv_gain,
    owner,
):
    ctx = lax.axis_index("ctx").astype(jnp.int32)
    tp = lax.axis_index("tp").astype(jnp.int32)
    level, core = tp // 2, tp % 2
    spare = BLK - beta_weight.shape[1]

    gathered = lax.all_gather(tokens, "tp", axis=0, tiled=True)
    rate_weight = jnp.pad(beta_weight, ((0, 0), (0, spare)))
    weights = jnp.concatenate([key_weight, values_projector_matrix, rate_weight], axis=1)
    bias = jnp.pad(beta_bias, (0, spare))[None]
    latent = latent_rows(tokens, kv_weight, kv_gain)
    tiles = jnp.stack([latent] + [turn(latent, "ctx", along_y(d)) for d in (1, 2, 3)])
    tiles = jnp.concatenate([tiles] + [turn(tiles, "ctx", along_x(d)) for d in (1, 2, 3)])
    cache = picked(tiles, owner, ctx)

    part = lax.dynamic_slice_in_dim(output_weight, ctx * 16, 16, 0)
    up, down = [part], [part]
    for s in range(4):
        up.append(turn(up[-1], "tp", along_z(1)))
        if s < 3:
            down.append(turn(down[-1], "tp", along_z(-1)))
    part = jnp.concatenate(up + down[:0:-1], axis=0)
    gathered = after(gathered, tiles, part, weights)
    all_parts = lax.all_gather(part, "ctx", axis=0, tiled=True)
    all_parts = all_parts.reshape(16, 8, 16, output_weight.shape[1])

    fallen, solved, states, maps, low = delta_blocks(dot(gathered, weights), log_decay, bias)
    z, y = rise(dot(gathered, query_weight), log_decay, fallen, solved, states)
    two, one, three = [turn(low, "ctx", along_y(d)) for d in (2, 1, 3)]
    before, total = side_maps((ctx % 4)[None], maps, (one, two, three))
    two, one, three = [turn(total, "ctx", down_x(d)) for d in (2, 1, 3)]
    gate = dot(gathered, gate_weight).astype(BF)
    info = jnp.stack([ctx // 4, level])
    normed = emit(info, before, total, (one, two, three), z, y, gate, head_gain[None], 8)

    passing = turn(normed[4], "tp", half_way())
    blocks = {0: normed[0], 4: passing}
    for d in (3, 5, 2):
        blocks[d] = turn(normed[d], "tp", along_z(d))
    blocks[8] = turn(passing, "tp", rest_of_way())
    for d in (6, 1, 7):
        blocks[d] = turn(after(normed[d], passing if d == 6 else blocks[8]), "tp", along_z(d))
    mine, theirs = output_rows(core[None], [blocks[d] for d in ARRIVAL], after(all_parts, cache))
    theirs = turn(theirs, "tp", across())
    return (mine + theirs.astype(F32)).astype(BF), cache


def solution(mesh):
    in_specs = (
        P(("ctx", "tp"), None),
        P(None, "tp"),
        P(None, "tp"),
        P(None, "tp"),
        P(None, "tp"),
        P(None, "tp"),
        P("tp"),
        P("ctx", "tp"),
        P(),
        P("tp", None),
        P(),
        P(),
        P(None, "tp"),
    )
    out_specs = (P(("ctx", "tp"), None), P("ctx", "tp", None))
    return jax.shard_map(body, mesh=mesh, in_specs=in_specs, out_specs=out_specs, check_vma=False)
```

```python
import functools
import jax
import jax.numpy as jnp
from jax import lax
from jax.experimental import pallas as pl
from jax.experimental.pallas import tpu as pltpu
from jax.sharding import PartitionSpec as P

BLK = 128
GUARD = 1e-06
BF = jnp.bfloat16
F32 = jnp.float32
VMEM_BYTES = 24 * 1024 * 1024


def dot(a, b, contract=((1,), (0,))):
    return lax.dot_general(a, b, (contract, ((), ())), preferred_element_type=F32)


def halves(a):
    high = a.astype(BF)
    return high, (a - high.astype(F32)).astype(BF)


def wide_left(a):
    return jnp.concatenate(halves(a), axis=1)


def wide_right(b):
    row = jnp.concatenate(halves(b), axis=1)
    return jnp.concatenate([row, row], axis=0)


def wide_dot(left, right):
    both = dot(left, right)
    n = both.shape[1] // 2
    return both[:, :n] + both[:, n:]


def indices(shape):
    return lax.broadcasted_iota(jnp.int32, shape, 0), lax.broadcasted_iota(jnp.int32, shape, 1)


def inverses(systems, row, col):
    eye = (row == col).astype(F32)
    joins = (row // 2 == col // 2) & (row > col)
    out = [eye - jnp.where(joins, s, 0.0) for s in systems]
    size = 2
    while size < BLK:
        joins = (row // (2 * size) == col // (2 * size)) & (row // size > col // size)
        parts = [jnp.where(joins, s, 0.0) for s in systems]
        lefts = [wide_left(t) for t in out]
        rights = [wide_right(t) for t in out]
        inner = [wide_dot(wide_left(p), r) for p, r in zip(parts, rights)]
        out = [t - wide_dot(l, wide_right(x)) for t, l, x in zip(out, lefts, inner)]
        size *= 2
    return out


def running(decay, ones):
    high = decay.astype(BF)
    rest = decay - high.astype(F32)
    mid = rest.astype(BF)
    low = (rest - mid.astype(F32)).astype(BF)
    both = dot(jnp.concatenate([ones, ones], axis=1), jnp.concatenate([high, mid], axis=0))
    return both + dot(ones, low)


def unit(rows):
    return rows * lax.rsqrt(jnp.sum(rows * rows, axis=-1, keepdims=True) + GUARD)


def delta_kernel(
    group, proj, ld, bias, k_out, w_out, s_out, x_out, low_out, rate, held
):
    first = pl.program_id(0) == 0
    lanes2 = 2 * BLK
    rate[...] = jax.nn.sigmoid(proj[:, 2 * lanes2 :] + bias[...])

    @pl.when(first)
    def start():
        across, along = indices((BLK, lanes2))
        for h in range(2):
            held[h] = (across == along).astype(F32)

    row, col = indices((BLK, BLK))
    ones = (row >= col).astype(BF)
    pairs = []
    for blk in range(group):
        at = slice(blk * BLK, (blk + 1) * BLK)
        decay = ld[at, :]
        cum = running(decay, ones)
        for h in range(2):
            lanes = slice(h * BLK, (h + 1) * BLK)
            pairs.append((blk, at, h, lanes, cum[:, lanes]))
    systems, targets, ends, finals = [], [], [], []
    for blk, at, h, lanes, c in pairs:
        k = unit(proj[at, lanes])
        v = proj[at, lanes2 + h * BLK : lanes2 + (h + 1) * BLK]
        beta = rate[at, h : h + 1]
        final = c[BLK - 1 : BLK, :]
        grow = jnp.exp(c)
        k_up = k * grow
        k_down = (k * jnp.exp(-c)).astype(BF)
        k_end = k * jnp.exp(final - c)
        k_out[at, lanes] = k_down
        gram = dot(k_up.astype(BF), k_down, ((1,), (1,)))
        systems.append(jnp.where(row > col, beta * gram, 0.0))
        targets.append(jnp.concatenate([(beta * k_up).astype(BF), (beta * v).astype(BF)], axis=1))
        ends.append(k_end.T.astype(BF))
        finals.append(jnp.exp(final))
    solved = inverses(systems, row, col)
    solved = [dot(t.astype(BF), g).astype(BF) for t, g in zip(solved, targets)]
    maps = {}
    for (blk, at, h, lanes, c), w_, e, last in zip(pairs, solved, ends, finals):
        w_out[blk, h] = w_
        both = dot(e, w_)
        m, n = jnp.where(row == col, last, 0.0) - both[:, :BLK], both[:, BLK:]
        maps[blk, h] = m, n
    joint = {}
    for pair in range(group // 2):
        for h in range(2):
            joint[pair, h] = follow(maps[2 * pair + 1, h], jnp.concatenate(maps[2 * pair, h], axis=1))
    x = [held[h] for h in range(2)]
    for pair in range(group // 2):
        for h in range(2):
            s_out[2 * pair, h] = x[h].astype(BF)
            s_out[2 * pair + 1, h] = follow(maps[2 * pair, h], x[h]).astype(BF)
            m, n = joint[pair, h][:, :BLK], joint[pair, h][:, BLK:]
            x[h] = follow((m, n), x[h])
    for h in range(2):
        held[h] = x[h]
        x_out[h] = x[h]
        low_out[h] = x[h].astype(BF)


def narrow_left(a):
    high, low = halves(a)
    return jnp.concatenate([high, low], axis=1), high


def compose(a, x):
    left, high = narrow_left(a)
    x_high, x_low = halves(x)
    return dot(left, jnp.concatenate([x_high, x_high], axis=0)) + dot(high, x_low)


def follow(step, x):
    moved = compose(step[0], x)
    return jnp.concatenate([moved[:, :BLK], moved[:, BLK:] + step[1]], axis=1)


def delta_blocks(projected, ld, bias, group=4):
    rows, width = projected.shape
    blocks = rows // BLK
    lanes = 2 * BLK
    tall = pl.BlockSpec((group * BLK, lanes), lambda i: (i, 0))
    square = pl.BlockSpec((group, 2, BLK, lanes), lambda i: (i, 0, 0, 0))
    last = pl.BlockSpec((2, BLK, lanes), lambda i: (0, 0, 0))
    return pl.pallas_call(
        functools.partial(delta_kernel, group),
        grid=(blocks // group,),
        in_specs=[
            pl.BlockSpec((group * BLK, width), lambda i: (i, 0)),
            tall,
            pl.BlockSpec(bias.shape, lambda i: (0, 0)),
        ],
        out_specs=[tall, square, square, last, last],
        out_shape=[
            jax.ShapeDtypeStruct((rows, lanes), BF),
            jax.ShapeDtypeStruct((blocks, 2, BLK, lanes), BF),
            jax.ShapeDtypeStruct((blocks, 2, BLK, lanes), BF),
            jax.ShapeDtypeStruct((2, BLK, lanes), F32),
            jax.ShapeDtypeStruct((2, BLK, lanes), BF),
        ],
        scratch_shapes=[
            pltpu.VMEM((group * BLK, BLK), F32),
            pltpu.VMEM((2, BLK, lanes), F32),
        ],
        compiler_params=pltpu.CompilerParams(vmem_limit_bytes=VMEM_BYTES),
        cost_estimate=pl.CostEstimate(
            flops=rows * 12 * 10**6, bytes_accessed=rows * 12000, transcendentals=0
        ),
        name="delta_blocks",
    )(projected, ld, bias)


def rise_kernel(group, q, ld, k, w, s, z_out, y_out):
    row, col = indices((BLK, BLK))
    ones = (row >= col).astype(BF)
    todo = [(j, h) for j in range(group) for h in range(2)]
    places = [(slice(j * BLK, (j + 1) * BLK), slice(h * BLK, (h + 1) * BLK)) for j, h in todo]
    grow = [jnp.exp(running(ld[j * BLK : (j + 1) * BLK], ones)) for j in range(group)]
    ups = [unit(q[p]) * grow[j][:, p[1]] for p, (j, h) in zip(places, todo)]
    grams = [dot(u.astype(BF), k[p], ((1,), (1,))) for u, p in zip(ups, places)]
    grams = [jnp.where(row >= col, g, 0.0).astype(BF) for g in grams]
    both = [dot(g, w[j, h]) for g, (j, h) in zip(grams, todo)]
    rises = [(u - b[:, :BLK]).astype(BF) for u, b in zip(ups, both)]
    for p, b, r, (j, h) in zip(places, both, rises, todo):
        seen = dot(r, s[j, h])
        z_out[p] = seen[:, :BLK].astype(BF)
        y_out[p] = seen[:, BLK:] + b[:, BLK:]


def rise(q, ld, k, w, s, group=4):
    rows, lanes = q.shape
    tall = pl.BlockSpec((group * BLK, lanes), lambda i: (i, 0))
    square = pl.BlockSpec((group,) + w.shape[1:], lambda i: (i, 0, 0, 0))
    return pl.pallas_call(
        functools.partial(rise_kernel, group),
        grid=(rows // (group * BLK),),
        in_specs=[tall, tall, tall, square, square],
        out_specs=[tall, tall],
        out_shape=[jax.ShapeDtypeStruct((rows, lanes), BF), jax.ShapeDtypeStruct((rows, lanes), F32)],
        compiler_params=pltpu.CompilerParams(vmem_limit_bytes=VMEM_BYTES),
        cost_estimate=pl.CostEstimate(
            flops=rows * 3 * 10**6, bytes_accessed=rows * 6000, transcendentals=0
        ),
        name="rise",
    )(q, ld, k, w, s)


def side_kernel(place, own, one, two, three, before, total, slots):
    me = place[0]
    for h in range(2):
        slots[0, h] = own[h]
        for d, got in enumerate((one, two, three)):
            slots[d + 1, h] = got[h].astype(F32)
    row, col = indices((BLK, 2 * BLK))
    maps = [None, None]
    for j in range(4):

        @pl.when(me == j)
        def keep():
            for h in range(2):
                before[h] = (row == col).astype(F32) if j == 0 else maps[h]

        at = (me + 4 - j) % 4
        for h in range(2):
            if j == 0:
                maps[h] = slots[at, h]
            else:
                moved = compose(slots[at, h, :, :BLK], maps[h])
                maps[h] = jnp.concatenate(
                    [moved[:, :BLK], moved[:, BLK:] + slots[at, h, :, BLK:]], axis=1
                )
    for h in range(2):
        total[h] = maps[h].astype(BF)


def side_maps(place, own, received):
    whole = pl.BlockSpec(own.shape, lambda i: (0, 0, 0))
    return pl.pallas_call(
        side_kernel,
        grid=(1,),
        in_specs=[pl.BlockSpec(memory_space=pltpu.SMEM)] + [whole] * 4,
        out_specs=[whole, whole],
        out_shape=[jax.ShapeDtypeStruct(own.shape, F32), jax.ShapeDtypeStruct(own.shape, BF)],
        scratch_shapes=[pltpu.VMEM((4,) + own.shape, F32)],
        compiler_params=pltpu.CompilerParams(vmem_limit_bytes=VMEM_BYTES),
        name="side_maps",
    )(place, own, *received)


def emit_kernel(together, info, before, own, one, two, three, gain, *refs):
    ins, outs, (slots, state) = refs[: 3 * together], refs[3 * together : -2], refs[-2:]
    me = info[0]

    @pl.when(pl.program_id(0) == 0)
    def enter():
        for d, got in enumerate((own, one, two, three)):
            slots[d] = got[...]
        for h in range(2):
            s = jnp.zeros((BLK, BLK), F32)
            for j in range(3):
                at = (me + 4 - j) % 4
                moved = slots[at, h, :, BLK:].astype(F32)
                if j > 0:
                    moved = moved + compose(slots[at, h, :, :BLK].astype(F32), s)
                s = jnp.where(j < me, moved, s)
            s = compose(before[h, :, :BLK], s) + before[h, :, BLK:]
            state[h] = s.astype(BF)

    made = []
    for z, y, gate in zip(*(ins[j * together : (j + 1) * together] for j in range(3))):
        done = []
        for h in range(2):
            lanes = slice(h * BLK, (h + 1) * BLK)
            a = y[:, lanes] + dot(z[:, lanes], state[h])
            scale = lax.rsqrt(jnp.mean(a * a, axis=-1, keepdims=True) + GUARD)
            a = a * scale * gain[...] * jax.nn.sigmoid(gate[:, lanes].astype(F32))
            done.append(a.astype(BF))
        made.append(jnp.concatenate(done, axis=1))
    for i in range(len(outs) // together):

        @pl.when(pl.program_id(0) == i)
        def put(i=i):
            for j, rows in enumerate(made):
                outs[i * together + j][...] = rows


def emit(info, before, own, received, z, y, gate, gain, levels, together=2):
    rows, lanes = z.shape
    rows //= levels
    small = pl.BlockSpec(own.shape, lambda i, info: (0, 0, 0))
    tall = [
        pl.BlockSpec((rows, lanes), lambda i, info, j=j: (lax.rem(info[1] + together * i + j, levels), 0))
        for j in range(together)
    ]
    return pl.pallas_call(
        functools.partial(emit_kernel, together),
        grid_spec=pltpu.PrefetchScalarGridSpec(
            num_scalar_prefetch=1,
            grid=(levels // together,),
            in_specs=[small] * 5 + [pl.BlockSpec((1, BLK), lambda i, info: (0, 0))] + tall * 3,
            out_specs=[pl.BlockSpec((rows, lanes), lambda i, info: (0, 0))] * levels,
            scratch_shapes=[pltpu.VMEM((4,) + own.shape, BF), pltpu.VMEM((2, BLK, BLK), BF)],
        ),
        out_shape=[jax.ShapeDtypeStruct((rows, lanes), BF)] * levels,
        compiler_params=pltpu.CompilerParams(vmem_limit_bytes=VMEM_BYTES),
        name="emit",
    )(info, before, own, *received, gain, *[z] * together, *[y] * together, *[gate] * together)


ARRIVAL = (0, 4, 3, 5, 2, 6, 8, 1, 7)


def output_kernel(info, *refs):
    blocks, (w, mine, theirs, total) = dict(zip(ARRIVAL, refs[:9])), refs[9:]
    core = info[0]
    parts, levels, rows, width = w.shape
    depth = parts * rows
    for i in range(levels):
        a = blocks[i][...]
        if i == 4:
            a = jnp.where(core == 0, a, blocks[8][...])
        more = dot(a, w[:, i].reshape(depth, width))
        total[...] = more if i == 0 else total[...] + more
    mine[...] = total[pl.ds(pl.multiple_of(core * BLK, BLK), BLK), :]
    theirs[...] = total[pl.ds(pl.multiple_of((1 - core) * BLK, BLK), BLK), :].astype(BF)


def output_rows(info, blocks, weight):
    parts, levels, rows, width = weight.shape
    here = pl.BlockSpec(memory_space=pltpu.VMEM)
    return pl.pallas_call(
        output_kernel,
        in_specs=[pl.BlockSpec(memory_space=pltpu.SMEM), here] + [here] * len(blocks),
        out_specs=[here, here],
        scratch_shapes=[
            pltpu.VMEM((2 * BLK, width), F32),
        ],
        out_shape=[
            jax.ShapeDtypeStruct((BLK, width), F32),
            jax.ShapeDtypeStruct((BLK, width), BF),
        ],
        compiler_params=pltpu.CompilerParams(vmem_limit_bytes=VMEM_BYTES),
        cost_estimate=pl.CostEstimate(
            flops=4 * BLK * parts * levels * rows * width,
            bytes_accessed=2 * parts * levels * rows * width,
            transcendentals=0,
        ),
        name="output_rows",
    )(info, *blocks, weight)


def turn(array, axis, pairs):
    return lax.ppermute(array, axis, pairs)


def along_y(d):
    return [(4 * x + y, 4 * x + (y + d) % 4) for x in range(4) for y in range(4)]


def down_x(d):
    return [(4 * x + y, 4 * (x + d) + y) for x in range(4 - d) for y in range(4)]


def along_x(d):
    return [(4 * x + y, 4 * ((x + d) % 4) + y) for x in range(4) for y in range(4)]


def across():
    return [(t, t ^ 1) for t in range(16)]


def along_z(d):
    return [(2 * z + k, 2 * ((z + d) % 8) + k) for z in range(8) for k in range(2)]


def after(array, *others):
    return lax.optimization_barrier((array,) + others)[0]


def half_way():
    return [(2 * z + k, 2 * ((z + 4 - 6 * k + 8) % 8) + k) for z in range(8) for k in range(2)]


def rest_of_way():
    return [(2 * z + 1, 2 * ((z + 6) % 8) + 1) for z in range(8)]


def latent_rows(tokens, kv_weight, kv_gain):
    latent = dot(tokens, kv_weight)
    scale = lax.rsqrt(jnp.mean(latent * latent, axis=-1, keepdims=True) + GUARD)
    return (latent * scale * kv_gain).astype(BF)


def pick_kernel(info, tile, out):
    out[...] = jnp.where(info[4 + pl.program_id(0)] > 0, tile[...], jnp.zeros_like(out))


def picked(tiles, owner, ctx):
    owners = owner.reshape(-1)
    count = owners.shape[0]
    order = jnp.arange(count, dtype=jnp.int32)
    same = owners[:, None] == owners[None, :]
    rank = jnp.sum((same & (order[None, :] < order[:, None])).astype(jnp.int32), axis=1)
    slots = jnp.arange(4, dtype=jnp.int32)[:, None]
    wanted = ((owners[None, :] == ctx) & (rank[None, :] == slots)).astype(jnp.int32)
    source = jnp.sum(wanted * order[None, :], axis=1)
    place = 4 * ((ctx // 4 - source // 4 + 4) % 4) + (ctx % 4 - source % 4 + 4) % 4
    info = jnp.concatenate([place, jnp.sum(wanted, axis=1)]).astype(jnp.int32)
    shape = tiles.shape[1:]
    return pl.pallas_call(
        pick_kernel,
        grid_spec=pltpu.PrefetchScalarGridSpec(
            num_scalar_prefetch=1,
            grid=(4,),
            in_specs=[pl.BlockSpec((1,) + shape, lambda i, info: (info[i], 0, 0))],
            out_specs=pl.BlockSpec((1,) + shape, lambda i, info: (i, 0, 0)),
        ),
        out_shape=jax.ShapeDtypeStruct((4,) + shape, tiles.dtype),
        compiler_params=pltpu.CompilerParams(vmem_limit_bytes=VMEM_BYTES),
        name="picked",
    )(info, tiles)


def body(
    tokens,
    query_weight,
    key_weight,
    values_projector_matrix,
    gate_weight,
    beta_weight,
    beta_bias,
    log_decay,
    head_gain,
    output_weight,
    kv_weight,
    kv_gain,
    owner,
):
    ctx = lax.axis_index("ctx").astype(jnp.int32)
    tp = lax.axis_index("tp").astype(jnp.int32)
    level, core = tp // 2, tp % 2
    spare = BLK - beta_weight.shape[1]

    gathered = lax.all_gather(tokens, "tp", axis=0, tiled=True)
    rate_weight = jnp.pad(beta_weight, ((0, 0), (0, spare)))
    weights = jnp.concatenate([key_weight, values_projector_matrix, rate_weight], axis=1)
    bias = jnp.pad(beta_bias, (0, spare))[None]
    latent = latent_rows(tokens, kv_weight, kv_gain)
    tiles = jnp.stack([latent] + [turn(latent, "ctx", along_y(d)) for d in (1, 2, 3)])
    tiles = jnp.concatenate([tiles] + [turn(tiles, "ctx", along_x(d)) for d in (1, 2, 3)])
    cache = picked(tiles, owner, ctx)

    part = lax.dynamic_slice_in_dim(output_weight, ctx * 16, 16, 0)
    up, down = [part], [part]
    for s in range(4):
        up.append(turn(up[-1], "tp", along_z(1)))
        if s < 3:
            down.append(turn(down[-1], "tp", along_z(-1)))
    part = jnp.concatenate(up + down[:0:-1], axis=0)
    gathered = after(gathered, tiles, part, weights)
    all_parts = lax.all_gather(part, "ctx", axis=0, tiled=True)
    all_parts = all_parts.reshape(16, 8, 16, output_weight.shape[1])

    fallen, solved, states, maps, low = delta_blocks(dot(gathered, weights), log_decay, bias)
    z, y = rise(dot(gathered, query_weight), log_decay, fallen, solved, states)
    two, one, three = [turn(low, "ctx", along_y(d)) for d in (2, 1, 3)]
    before, total = side_maps((ctx % 4)[None], maps, (one, two, three))
    two, one, three = [turn(total, "ctx", down_x(d)) for d in (2, 1, 3)]
    gate = dot(gathered, gate_weight).astype(BF)
    info = jnp.stack([ctx // 4, level])
    normed = emit(info, before, total, (one, two, three), z, y, gate, head_gain[None], 8)

    passing = turn(normed[4], "tp", half_way())
    blocks = {0: normed[0], 4: passing}
    for d in (3, 5, 2, 6, 1, 7):
        blocks[d] = turn(normed[d], "tp", along_z(d))
    blocks[8] = turn(passing, "tp", rest_of_way())
    mine, theirs = output_rows(core[None], [blocks[d] for d in ARRIVAL], after(all_parts, cache))
    theirs = turn(theirs, "tp", across())
    return (mine + theirs.astype(F32)).astype(BF), cache


def solution(mesh):
    in_specs = (
        P(("ctx", "tp"), None),
        P(None, "tp"),
        P(None, "tp"),
        P(None, "tp"),
        P(None, "tp"),
        P(None, "tp"),
        P("tp"),
        P("ctx", "tp"),
        P(),
        P("tp", None),
        P(),
        P(),
        P(None, "tp"),
    )
    out_specs = (P(("ctx", "tp"), None), P("ctx", "tp", None))
    return jax.shard_map(body, mesh=mesh, in_specs=in_specs, out_specs=out_specs, check_vma=False)
```
